256 devices in a mesh: dom: 64 (over x, z, core), hid: 4 (over y).
Axes of the slice: x: 4, y: 4, z: 8, core: 2. Of those that a mesh axis runs over, the one named last changes fastest.
Arguments:
- feat: bfloat16 [16384, 1024], P('dom', 'hid'), may hold values from -6 to 6
- cotangent: bfloat16 [16384, 1024], P('dom', 'hid'), may hold values from -6 to 6
- tiles: bfloat16 [64, 32, 128, 128], P('dom')
- tile_index: int32 [64, 32], P('dom'), may hold values from 0 to 35, as said below
- tile_count: int32 [64], P('dom'), may hold values from 6 to 32, as said below
- replica_slot: int32 [64, 512], P('dom'), may hold values from 0 to 255, as said below
- recv_count: int32 [64, 64], P('dom'), may hold values from 0 to 8, as said below
- w_self1: bfloat16 [1024, 1024], P(None, 'hid'), may hold values from -0.1875 to 0.1875
- w_neigh1: bfloat16 [1024, 1024], P(None, 'hid'), may hold values from -0.1875 to 0.1875
- w_self2: bfloat16 [1024, 1024], P(None, 'hid'), may hold values from -0.1875 to 0.1875
- w_neigh2: bfloat16 [1024, 1024], P(None, 'hid'), may hold values from -0.1875 to 0.1875
Outputs:
- output: bfloat16 [16384, 1024], P('dom', 'hid')
- grad_self1: float32 [1024, 1024], P(None, 'hid')
- grad_neigh1: float32 [1024, 1024], P(None, 'hid')
- grad_self2: float32 [1024, 1024], P(None, 'hid')
- grad_neigh2: float32 [1024, 1024], P(None, 'hid')
The draws below stay inside these ranges and needn't reach their ends.
Inputs may be any that keep to these rules, and one draw needn't show every extreme that they name: `tile_index`: entries of one partition are distinct; entry e names the tile at block row e // 6 and block column e % 6; the first 6 entries of every partition are its diagonal tiles in some order. Partition d uses its first tile_count[d] tile slots; some partition uses all 32. `replica_slot`: entry p * 8 + c of owner d is the master row held in mirror slot c of partition p; the 8 entries for one partition are distinct. `recv_count`: entry [d, p] says how many of the first mirror slots for owner d on partition p are live; it is zero for p = d, and every owner has a partition with all 8 live.
All inputs are finite; a program needn't handle non-finite values.
Results may differ from the reference program's by a relative error of at most 0.0058.
Values may be sent and summed in bfloat16 or wider, within the bound.
A program may use at most 64 MiB of HBM per device.

```python
import math
import jax
import jax.numpy as jnp
from jax import lax

WIDTH = 1024
TILE = 128
MASTERS = 256
TILES = 32
SLOTS = 8
BLOCKS = 6
VERTICES = 16384
N_DOM = 64


def draw_tiles(key, part):
    key = jax.random.fold_in(key, 15)
    mask_key, value_key = jax.random.split(key)
    dims = (N_DOM, TILES, TILE, TILE)
    present = jax.random.uniform(mask_key, dims, jnp.float32) < 0.35
    values = jax.random.uniform(value_key, dims, jnp.float32, 0.5, 1.5)
    per_row = (BLOCKS + TILES // 2) / (2.0 * BLOCKS)
    scaling = 1.0 / math.sqrt(0.35 * 1.08 * TILE * per_row)
    return jnp.where(present, values * scaling, 0.0).astype(jnp.bfloat16)


def draw_tile_index(key, part):
    key = jax.random.fold_in(key, 11)
    off_count = BLOCKS * (BLOCKS - 1)
    ordinal = jnp.arange(off_count, dtype=jnp.int32)
    row_part = ordinal // (BLOCKS - 1)
    shifted = ordinal % (BLOCKS - 1)
    col_part = shifted + (shifted >= row_part).astype(jnp.int32)
    off_diagonal = row_part * BLOCKS + col_part
    diagonal = jnp.arange(BLOCKS, dtype=jnp.int32) * (BLOCKS + 1)

    def one_partition(sub_key):
        first_key, second_key = jax.random.split(sub_key)
        leading = jax.random.permutation(first_key, diagonal)
        remaining = jax.random.permutation(second_key, off_diagonal)[:TILES - BLOCKS]
        return jnp.concatenate([leading, remaining]).astype(jnp.int32)
    return jax.vmap(one_partition)(jax.random.split(key, N_DOM))


def draw_tile_count(key, part):
    key = jax.random.fold_in(key, 12)
    count_key, pick_key = jax.random.split(key)
    counts = jax.random.randint(count_key, (N_DOM,), BLOCKS, TILES // 2 + 1, dtype=jnp.int32)
    chosen = jax.random.randint(pick_key, (), 0, N_DOM, dtype=jnp.int32)
    return jnp.where(jnp.arange(N_DOM, dtype=jnp.int32) == chosen, TILES, counts).astype(jnp.int32)


def draw_replica_slot(key, part):
    key = jax.random.fold_in(key, 13)
    keys_all = jax.random.split(key, N_DOM * N_DOM)
    picked = jax.vmap(lambda sub_key: jax.random.permutation(sub_key, MASTERS)[:SLOTS])(keys_all)
    return picked.reshape(N_DOM, N_DOM * SLOTS).astype(jnp.int32)


def draw_recv_count(key, part):
    key = jax.random.fold_in(key, 14)
    base_key, full_key = jax.random.split(key)
    counts = jax.random.randint(base_key, (N_DOM, N_DOM), SLOTS // 2, SLOTS + 1, dtype=jnp.int32)
    offset = jax.random.randint(full_key, (N_DOM,), 1, N_DOM, dtype=jnp.int32)
    owners = jnp.arange(N_DOM, dtype=jnp.int32)
    full_peer = (owners + offset) % N_DOM
    counts = jnp.where(owners[None, :] == full_peer[:, None], SLOTS, counts)
    counts = jnp.where(owners[:, None] == owners[None, :], 0, counts)
    return counts.astype(jnp.int32)


def shard_levels(stream_key, extent, cuts, low, top_value):
    factor_of, own = 1.0, jax.random.fold_in(stream_key, 6)
    for dim, parts in cuts:
        steps = jnp.exp(jax.random.uniform(jax.random.fold_in(own, dim), (parts,), jnp.float32, low / len(cuts), top_value / len(cuts)))
        factor_of = factor_of * jnp.repeat(steps, extent[dim] // parts).reshape([-1 if axis == dim else 1 for axis in range(len(extent))])
    return factor_of


def bell_draw(stream_key, shape, scale, reach, cuts=(), kind=jnp.bfloat16):
    drawn = scale * jax.random.normal(stream_key, shape, jnp.float32)
    if cuts:
        drawn = drawn * shard_levels(stream_key, shape, cuts, -0.22, 0.18)
    return jnp.clip(drawn, -reach, reach).astype(kind)


def setup_inputs(seed: int = 0) -> dict:
    keys = jax.random.split(jax.random.key(seed), 12)
    return {
        "feat": bell_draw(keys[0], (VERTICES, WIDTH), 1.0, 6.0, ((0, 64), (1, 4))),
        "cotangent": bell_draw(keys[1], (VERTICES, WIDTH), 1.0, 6.0, ((0, 64), (1, 4))),
        "tiles": draw_tiles(jax.random.fold_in(keys[11], 71), 0),
        "tile_index": draw_tile_index(jax.random.fold_in(keys[11], 71), 0),
        "tile_count": draw_tile_count(jax.random.fold_in(keys[11], 71), 0),
        "replica_slot": draw_replica_slot(jax.random.fold_in(keys[11], 71), 0),
        "recv_count": draw_recv_count(jax.random.fold_in(keys[11], 71), 0),
        "w_self1": bell_draw(keys[7], (WIDTH, WIDTH), WIDTH ** -0.5, 0.1875, ((1, 4),)),
        "w_neigh1": bell_draw(keys[8], (WIDTH, WIDTH), WIDTH ** -0.5, 0.1875, ((1, 4),)),
        "w_self2": bell_draw(keys[9], (WIDTH, WIDTH), WIDTH ** -0.5, 0.1875, ((1, 4),)),
        "w_neigh2": bell_draw(keys[10], (WIDTH, WIDTH), WIDTH ** -0.5, 0.1875, ((1, 4),)),
    }


def propagate(local_field, tile_values, tile_slots, tile_total, transpose):
    block_count = local_field.shape[0] // TILE
    width_all = local_field.shape[1]
    blocked = local_field.astype(jnp.float32).reshape(block_count, TILE, width_all)
    block_rows = tile_slots // block_count
    block_cols = tile_slots % block_count
    active = (jnp.arange(TILES, dtype=jnp.int32) < tile_total).astype(jnp.float32)
    weights_full = tile_values.astype(jnp.float32)
    if transpose:
        product = jnp.einsum('tji,tjq->tiq', weights_full, blocked[block_rows], precision=lax.Precision.HIGHEST)
        target = block_cols
    else:
        product = jnp.einsum('tij,tjq->tiq', weights_full, blocked[block_cols], precision=lax.Precision.HIGHEST)
        target = block_rows
    product = product * active[:, None, None]
    result = jnp.zeros((block_count, TILE, width_all), jnp.float32).at[target].add(product)
    return result.reshape(block_count * TILE, width_all)

def spread(masters3, replica_slot, recv_count):
    groups = masters3.shape[0]
    slot_table = replica_slot.reshape(groups, groups, SLOTS)
    live_table = jnp.arange(SLOTS, dtype=jnp.int32)[None, None, :] < recv_count[:, :, None]
    owners = jnp.arange(groups, dtype=jnp.int32)

    def for_holder(holder):
        picked = masters3[owners[:, None], slot_table[:, holder, :]]
        picked = jnp.where(live_table[:, holder, :, None], picked, jnp.zeros((), masters3.dtype))
        return picked.reshape(groups * SLOTS, masters3.shape[2])
    return lax.map(for_holder, owners)

def collect(master_part, mirror_part, replica_slot, recv_count):
    groups = master_part.shape[0]
    slot_table = replica_slot.reshape(groups, groups, SLOTS)
    live_table = jnp.arange(SLOTS, dtype=jnp.int32)[None, None, :] < recv_count[:, :, None]

    def for_owner(owner):
        pieces = lax.dynamic_slice_in_dim(mirror_part, owner * SLOTS, SLOTS, 1)
        pieces = jnp.where(live_table[owner][:, :, None], pieces.astype(jnp.float32), jnp.zeros((), jnp.float32))
        return master_part[owner].at[slot_table[owner].reshape(-1)].add(pieces.reshape(groups * SLOTS, -1))
    return lax.map(for_owner, jnp.arange(groups, dtype=jnp.int32))

def aggregate(masters3, tiles, tile_index, tile_count, replica_slot, recv_count, transpose):
    mirror_rows = spread(masters3, replica_slot, recv_count)

    def per_device(packed):
        own_rows, held_rows, tile_values, tile_slots, tile_total = packed
        local_field = jnp.concatenate([own_rows, held_rows], axis=0)
        partial_sum = propagate(local_field, tile_values, tile_slots, tile_total, transpose)
        return (partial_sum[:MASTERS], partial_sum[MASTERS:].astype(jnp.bfloat16))
    master_part, mirror_part = lax.map(per_device, (masters3, mirror_rows, tiles, tile_index, tile_count))
    summed = collect(master_part, mirror_part, replica_slot, recv_count)
    return summed.reshape(VERTICES, masters3.shape[2])

def reference(feat, cotangent, tiles, tile_index, tile_count, replica_slot, recv_count, w_self1, w_neigh1, w_self2, w_neigh2):
    shape_three = (N_DOM, MASTERS, WIDTH)
    agg_one = aggregate(feat.reshape(shape_three), tiles, tile_index, tile_count, replica_slot, recv_count, False).astype(jnp.bfloat16)
    pre_one = jnp.dot(feat, w_self1, preferred_element_type=jnp.float32) + jnp.dot(agg_one, w_neigh1, preferred_element_type=jnp.float32)
    hidden_one = jax.nn.silu(pre_one).astype(jnp.bfloat16)
    agg_two = aggregate(hidden_one.reshape(shape_three), tiles, tile_index, tile_count, replica_slot, recv_count, False).astype(jnp.bfloat16)
    pre_two = jnp.dot(hidden_one, w_self2, preferred_element_type=jnp.float32) + jnp.dot(agg_two, w_neigh2, preferred_element_type=jnp.float32)
    output = pre_two.astype(jnp.bfloat16)
    factor = 1.0 / math.sqrt(VERTICES)
    grad_self2 = jnp.dot(hidden_one.T, cotangent, preferred_element_type=jnp.float32) * factor
    grad_neigh2 = jnp.dot(agg_two.T, cotangent, preferred_element_type=jnp.float32) * factor
    back_hidden = jnp.dot(cotangent, w_self2.T, preferred_element_type=jnp.float32).astype(jnp.bfloat16)
    back_agg = jnp.dot(cotangent, w_neigh2.T, preferred_element_type=jnp.float32).astype(jnp.bfloat16)
    back_hidden = lax.optimization_barrier(back_hidden)
    adjoint = aggregate(back_agg.reshape(shape_three), tiles, tile_index, tile_count, replica_slot, recv_count, True)
    back_one = back_hidden.astype(jnp.float32) + adjoint
    sigma = jax.nn.sigmoid(pre_one)
    back_pre = (back_one * sigma * (1.0 + pre_one * (1.0 - sigma))).astype(jnp.bfloat16)
    grad_self1 = jnp.dot(feat.T, back_pre, preferred_element_type=jnp.float32) * factor
    grad_neigh1 = jnp.dot(agg_one.T, back_pre, preferred_element_type=jnp.float32) * factor
    return (output, grad_self1, grad_neigh1, grad_self2, grad_neigh2)
```

```python
import math

import jax
import jax.numpy as jnp
from jax import lax
from jax.experimental import pallas as pl
from jax.experimental.pallas import tpu as pltpu
from jax.sharding import PartitionSpec as P

BF = jnp.bfloat16
F32 = jnp.float32
I32 = jnp.int32
LANES = 128
CHIPS_Z = 8


def dot(a, b):
    return jnp.dot(a, b, preferred_element_type=F32)


def dot_t(a, b):
    return lax.dot_general(a, b, (((0,), (0,)), ((), ())), preferred_element_type=F32)


def dot_r(a, b):
    return lax.dot_general(a, b, (((1,), (1,)), ((), ())), preferred_element_type=F32)


def pack(rows, slots):
    count, width = rows.shape
    parts = [
        rows[:, i : i + LANES].reshape(count // slots, slots, LANES) for i in range(0, width, LANES)
    ]
    return jnp.concatenate(parts, axis=1).astype(BF)


def unpack(packed, slots):
    wide = packed.astype(F32)
    groups, rows, _ = wide.shape
    parts = [
        wide[:, i : i + slots, :].reshape(groups * slots, LANES) for i in range(0, rows, slots)
    ]
    return jnp.concatenate(parts, axis=1).astype(BF)


def kernel(
    dims,
    slot_of,
    used,
    feat,
    cot,
    slot_row,
    counts,
    tiles,
    ws1,
    wn1,
    ws2,
    wn2,
    out,
    gout,
    tiles_v,
    w_v,
    onehot,
    onehot_t,
    adj,
    adj_t,
    send1,
    recv1,
    send2,
    recv2,
    send3,
    recv3,
    send4,
    recv4,
    left,
    hid_all,
    right,
    back_f32,
    rs_send,
    rs_recv,
    pre_v,
    own_v,
    acc,
    s0s,
    s0r,
    s1s,
    s1r,
    own1,
    s2s,
    s2r,
    fin,
    lsem,
    esem,
    ersem,
    ysem,
    yrsem,
    gsem,
    grsem,
):
    doms, hids, slots, masters, narrow = dims
    chips_z = CHIPS_Z
    chips_x = doms // (2 * chips_z)
    size = tiles.shape[1]
    mirrors = doms * slots
    blocks = (masters + mirrors) // size
    width = hids * narrow
    me = lax.axis_index("dom")
    hid = lax.axis_index("hid")
    core = lax.rem(me, 2)
    chip = me // 2
    cx, cz = chip // chips_z, lax.rem(chip, chips_z)

    def remote(src, dst, ssem, rsem, **where):
        return pltpu.make_async_remote_copy(
            src_ref=src,
            dst_ref=dst,
            send_sem=ssem,
            recv_sem=rsem,
            device_id=where,
            device_id_type=pl.DeviceIdType.MESH,
        )

    barrier = pltpu.get_barrier_semaphore()

    def greet(i, carry):
        pl.semaphore_signal(
            barrier,
            inc=1,
            device_id={"dom": lax.rem(me + i, doms)},
            device_id_type=pl.DeviceIdType.MESH,
        )
        return carry

    lax.fori_loop(1, doms, greet, 0)
    for i in range(1, hids):
        pl.semaphore_signal(
            barrier,
            inc=1,
            device_id={"hid": lax.rem(hid + i, hids)},
            device_id_type=pl.DeviceIdType.MESH,
        )

    loads = [pltpu.make_async_copy(tiles, tiles_v, lsem.at[0])]
    for i, w in enumerate((ws1, ws2, wn1, wn2)):
        loads.append(pltpu.make_async_copy(w, w_v.at[i], lsem.at[i + 1]))
    for load in loads:
        load.start()

    grp = lax.broadcasted_iota(I32, (doms, mirrors), 0)
    col = lax.broadcasted_iota(I32, (doms, mirrors), 1)
    repeat = (col // slots == grp).astype(F32)
    live_count = dot(jnp.broadcast_to(counts[...].astype(F32), (8, doms)), repeat)[0:1]
    lane = lax.broadcasted_iota(I32, (1, mirrors), 1)
    live = lax.rem(lane, slots).astype(F32) + 0.5 < live_count
    slot = jnp.where(live, slot_row[...], -1)
    row = lax.broadcasted_iota(I32, (masters, mirrors), 0)
    hot = (row == slot).astype(F32)
    onehot_t[...] = hot.astype(BF)
    onehot[...] = hot.T.astype(BF)

    send1[...] = pack(dot(onehot[...], jnp.concatenate([feat[...], cot[...]], axis=1)), slots)
    for buf in (recv1, recv2, recv3, recv4):
        buf[me] = jnp.zeros(buf.shape[1:], BF)
    left[0, hid] = feat[...]
    right[0] = cot[...]

    pl.semaphore_wait(barrier, doms - 1 + hids - 1)

    def exchange_start(n, src, dst):
        def one(i, carry):
            peer = lax.rem(me + i, doms)
            remote(src.at[peer], dst.at[me], esem.at[n], ersem.at[n], dom=peer).start()
            return carry

        lax.fori_loop(1, doms, one, 0)

    def exchange_wait(n, src, dst):
        some = pl.ds(0, doms - 1)
        done = remote(
            src.at[some], dst.at[some], esem.at[n], ersem.at[n], dom=lax.rem(me + 1, doms)
        )
        done.wait_recv()
        done.wait_send()

    def gather_start(n, src, dst):
        for i in range(1, hids):
            remote(src, dst, ysem.at[n], yrsem.at[n], hid=lax.rem(hid + i, hids)).start()

    def gather_wait(n, src, dst):
        some = pl.ds(0, hids - 1)
        done = remote(src.at[some], dst.at[some], ysem.at[n], yrsem.at[n], hid=lax.rem(hid + 1, hids))
        done.wait_recv()
        done.wait_send()

    exchange_start(0, send1, recv1)
    gather_start(0, feat, left.at[0, hid])

    loads[0].wait()
    for r in range(blocks):
        for c in range(blocks):
            e = r * blocks + c
            tile = jnp.where(used[e] > 0, tiles_v[slot_of[e]], jnp.zeros((), BF))
            rs, cs = pl.ds(r * size, size), pl.ds(c * size, size)
            adj[rs, cs] = tile
            adj_t[cs, rs] = tile.astype(F32).T.astype(BF)

    for load in loads[1:]:
        load.wait()

    def block(h):
        return pl.ds(h * narrow, narrow)

    for h in range(hids):
        back_f32[h] = dot_r(cot[...], w_v[1, block(h)])

    top, low = pl.ds(0, masters), pl.ds(masters, mirrors)
    exchange_wait(0, send1, recv1)
    held = unpack(recv1[...], slots)
    fwd, bwd = held[:, :narrow], held[:, narrow:]
    mirror = jnp.concatenate(
        [
            dot(adj[low, top], feat[...]) + dot(adj[low, low], fwd),
            dot(adj_t[low, top], cot[...]) + dot(adj_t[low, low], bwd),
        ],
        axis=1,
    )
    send2[...] = pack(mirror, slots)
    exchange_start(1, send2, recv2)
    own_v[0] = dot(adj[top, top], feat[...]) + dot(adj[top, low], fwd)
    own_v[1] = dot(adj_t[top, top], cot[...]) + dot(adj_t[top, low], bwd)

    gather_wait(0, left.at[0], left.at[0])
    pre = dot(left[0, 0], w_v[0, block(0)])
    for h in range(1, hids):
        pre += dot(left[0, h], w_v[0, block(h)])
    pre_v[...] = pre

    exchange_wait(1, send2, recv2)
    back = unpack(recv2[...], slots)
    left[1, hid] = (own_v[0] + dot(onehot_t[...], back[:, :narrow])).astype(BF)
    gather_start(1, left.at[1, hid], left.at[1, hid])
    right[1] = (own_v[1] + dot(onehot_t[...], back[:, narrow:])).astype(BF)
    for h in range(hids):
        rs_send[h] = (back_f32[h] + dot_r(right[1], w_v[3, block(h)])).astype(BF)
    for i in range(1, hids):
        peer = lax.rem(hid + i, hids)
        remote(rs_send.at[peer], rs_recv.at[hid], ysem.at[2], yrsem.at[2], hid=peer).start()

    gather_wait(1, left.at[1], left.at[1])
    pre = pre_v[...]
    for h in range(hids):
        pre += dot(left[1, h], w_v[2, block(h)])
    sigma = jax.nn.sigmoid(pre)
    hid_all[hid] = (pre * sigma).astype(BF)
    gather_start(3, hid_all.at[hid], hid_all.at[hid])

    gather_wait(2, rs_send, rs_recv)
    back_one = rs_send[hid].astype(F32)
    for i in range(1, hids):
        back_one += rs_recv[lax.rem(hid + i, hids)].astype(F32)
    back_pre = (back_one * sigma * (1.0 + pre * (1.0 - sigma))).astype(BF)

    sibling = me + 1 - 2 * core
    piece = width // chips_x
    chunk = piece // chips_z
    factor = 1.0 / math.sqrt(doms * masters)

    def to_sibling(g):
        return remote(s0s.at[g], s0r.at[g], gsem.at[g, 0], grsem.at[g, 0], dom=sibling)

    for h in range(hids):
        s0s[0, block(h)] = dot_t(left[1 - core, h], back_pre).astype(BF)
    to_sibling(0).start()
    for h in range(hids):
        acc[0, block(h)] = dot_t(left[core, h], back_pre)

    gather_wait(3, hid_all, hid_all)
    mixed = dot(hid_all[0], w_v[3, block(0)])
    for h in range(1, hids):
        mixed += dot(hid_all[h], w_v[3, block(h)])
    mixed = mixed.astype(BF)
    send3[...] = pack(dot(onehot[...], mixed), slots)
    exchange_start(2, send3, recv3)

    for h in range(hids):
        s0s[1, block(h)] = dot_t(hid_all[h], right[1 - core]).astype(BF)
    to_sibling(1).start()
    for h in range(hids):
        acc[1, block(h)] = dot_t(hid_all[h], right[core])

    def dom_of(x, z):
        return (x * chips_z + z) * 2 + core

    def x_start(g):
        done = to_sibling(g)
        done.wait_recv()
        done.wait_send()
        s1s[g] = (acc[g] + s0r[g].astype(F32)).astype(BF)
        mine = pl.ds(cx * piece, piece)
        own1[g] = acc[g, mine] + s0r[g, mine].astype(F32)
        for i in range(1, chips_x):
            px = lax.rem(cx + i, chips_x)
            remote(
                s1s.at[g, pl.ds(px * piece, piece)],
                s1r.at[g, cx],
                gsem.at[g, 1],
                grsem.at[g, 1],
                dom=dom_of(px, cz),
            ).start()

    def z_start(g):
        some = pl.ds(0, (chips_x - 1) * piece)
        done = remote(
            s1s.at[g, some], s1s.at[g, some], gsem.at[g, 1], grsem.at[g, 1], dom=sibling
        )
        done.wait_recv()
        done.wait_send()
        total = own1[g]
        for i in range(1, chips_x):
            total += s1r[g, lax.rem(cx + i, chips_x)].astype(F32)
        own1[g] = total
        s2s[g] = total.astype(BF)
        for i in range(1, chips_z):
            pz = lax.rem(cz + i, chips_z)
            remote(
                s2s.at[g, pl.ds(pz * chunk, chunk)],
                s2r.at[g, cz],
                gsem.at[g, 2],
                grsem.at[g, 2],
                dom=dom_of(cx, pz),
            ).start()

    def z_back(g):
        some = pl.ds(0, (chips_z - 1) * chunk)
        done = remote(
            s2s.at[g, some], s2s.at[g, some], gsem.at[g, 2], grsem.at[g, 2], dom=sibling
        )
        done.wait_recv()
        done.wait_send()
        total = own1[g, pl.ds(cz * chunk, chunk)]
        for i in range(1, chips_z):
            total += s2r[g, lax.rem(cz + i, chips_z)].astype(F32)
        fin[g] = (total * factor).astype(BF)
        place = gout.at[g, core, pl.ds(cx * piece + cz * chunk, chunk)]
        pltpu.make_async_copy(fin.at[g], place, lsem.at[5 + g]).start()
        for i in range(1, chips_z):
            pz = lax.rem(cz + i, chips_z)
            remote(fin.at[g], place, gsem.at[g, 3], grsem.at[g, 3], dom=dom_of(cx, pz)).start()

    def x_back(g):
        place = gout.at[g, core, pl.ds(cx * piece + cz * chunk, chunk)]
        pltpu.make_async_copy(fin.at[g], place, lsem.at[5 + g]).wait()
        some = gout.at[g, core, pl.ds(0, (chips_z - 1) * chunk)]
        done = remote(some, some, gsem.at[g, 3], grsem.at[g, 3], dom=sibling)
        done.wait_recv()
        done.wait_send()
        mine = gout.at[g, core, pl.ds(cx * piece, piece)]
        for i in range(1, chips_x):
            px = lax.rem(cx + i, chips_x)
            remote(mine, mine, gsem.at[g, 4], grsem.at[g, 4], dom=dom_of(px, cz)).start()

    def core_back(g):
        some = gout.at[g, core, pl.ds(0, (chips_x - 1) * piece)]
        done = remote(some, some, gsem.at[g, 4], grsem.at[g, 4], dom=sibling)
        done.wait_recv()
        done.wait_send()
        mine = gout.at[g, core]
        remote(mine, mine, gsem.at[g, 5], grsem.at[g, 5], dom=sibling).start()

    x_start(0)

    exchange_wait(2, send3, recv3)
    held = unpack(recv3[...], slots)
    send4[...] = pack(dot(adj[low, top], mixed) + dot(adj[low, low], held), slots)
    exchange_start(3, send4, recv4)
    x_start(1)
    total = dot(adj[top, top], mixed) + dot(adj[top, low], held)
    for h in range(hids):
        total += dot(hid_all[h], w_v[1, block(h)])
    own_v[0] = total

    z_start(0)
    z_back(0)
    exchange_wait(3, send4, recv4)
    out[...] = (own_v[0] + dot(onehot_t[...], unpack(recv4[...], slots))).astype(BF)
    z_start(1)
    x_back(0)
    z_back(1)
    core_back(0)
    x_back(1)
    core_back(1)
    for g in range(2):
        mine = gout.at[g, core]
        done = remote(mine, mine, gsem.at[g, 5], grsem.at[g, 5], dom=sibling)
        done.wait_recv()
        done.wait_send()


def local(
    feat,
    cotangent,
    tiles,
    tile_index,
    tile_count,
    replica_slot,
    recv_count,
    w_self1,
    w_neigh1,
    w_self2,
    w_neigh2,
):
    doms, hids = lax.axis_size("dom"), lax.axis_size("hid")
    masters, narrow = feat.shape
    width = narrow * hids
    mirrors = replica_slot.shape[1]
    slots = mirrors // doms
    size = tiles.shape[2]
    blocks = (masters + mirrors) // size
    side = blocks * size
    chips_x = doms // (2 * CHIPS_Z)
    piece = width // chips_x
    chunk = piece // CHIPS_Z

    order = jnp.arange(tiles.shape[1], dtype=I32)
    match = (
        (tile_index[0][None, :] == jnp.arange(blocks * blocks, dtype=I32)[:, None])
        & (order < tile_count[0])[None, :]
    ).astype(I32)
    slot_of = (match * order[None, :]).sum(axis=1)
    used = match.sum(axis=1)

    packed = slots * narrow // LANES
    smem = pl.BlockSpec(memory_space=pltpu.SMEM)
    vmem = pl.BlockSpec(memory_space=pltpu.VMEM)
    anym = pl.BlockSpec(memory_space=pl.ANY)
    dma = pltpu.SemaphoreType.DMA

    def body(*refs):
        kernel((doms, hids, slots, masters, narrow), *refs)

    out, grads = pl.pallas_call(
        body,
        out_shape=(
            jax.ShapeDtypeStruct((masters, narrow), BF),
            jax.ShapeDtypeStruct((2, 2, width, narrow), BF),
        ),
        in_specs=[smem] * 2 + [vmem] * 4 + [anym] * 5,
        out_specs=(vmem, anym),
        scratch_shapes=[
            pltpu.VMEM(tiles.shape[1:], BF),
            pltpu.VMEM((4, width, narrow), BF),
            pltpu.VMEM((mirrors, masters), BF),
            pltpu.VMEM((masters, mirrors), BF),
            pltpu.VMEM((side, side), BF),
            pltpu.VMEM((side, side), BF),
        ]
        + [pltpu.VMEM((doms, 2 * packed, LANES), BF)] * 4
        + [pltpu.VMEM((doms, packed, LANES), BF)] * 4
        + [
            pltpu.VMEM((2, hids, masters, narrow), BF),
            pltpu.VMEM((hids, masters, narrow), BF),
            pltpu.VMEM((2, masters, narrow), BF),
            pltpu.VMEM((hids, masters, narrow), F32),
            pltpu.VMEM((hids, masters, narrow), BF),
            pltpu.VMEM((hids, masters, narrow), BF),
            pltpu.VMEM((masters, narrow), F32),
            pltpu.VMEM((2, masters, narrow), F32),
            pltpu.VMEM((2, width, narrow), F32),
            pltpu.VMEM((2, width, narrow), BF),
            pltpu.VMEM((2, width, narrow), BF),
            pltpu.VMEM((2, width, narrow), BF),
            pltpu.VMEM((2, chips_x, piece, narrow), BF),
            pltpu.VMEM((2, piece, narrow), F32),
            pltpu.VMEM((2, piece, narrow), BF),
            pltpu.VMEM((2, CHIPS_Z, chunk, narrow), BF),
            pltpu.VMEM((2, chunk, narrow), BF),
            dma((7,)),
            dma((4,)),
            dma((4,)),
            dma((4,)),
            dma((4,)),
            dma((2, 6)),
            dma((2, 6)),
        ],
        compiler_params=pltpu.CompilerParams(
            collective_id=0, has_side_effects=True, vmem_limit_bytes=48 * 1024 * 1024
        ),
    )(
        slot_of,
        used,
        feat,
        cotangent,
        replica_slot,
        recv_count,
        tiles[0],
        w_self1,
        w_neigh1,
        w_self2,
        w_neigh2,
    )
    grads = grads.astype(F32)
    return (out, grads[0, 0], grads[0, 1], grads[1, 0], grads[1, 1])


def solution(mesh):
    rows = P("dom", "hid")
    cols = P(None, "hid")
    return jax.shard_map(
        local,
        mesh=mesh,
        in_specs=(
            rows,
            rows,
            P("dom", None, None, None),
            P("dom", None),
            P("dom"),
            P("dom", None),
            P("dom", None),
            cols,
            cols,
            cols,
            cols,
        ),
        out_specs=(rows, cols, cols, cols, cols),
        check_vma=False,
    )
```

```python
import math

import jax
import jax.numpy as jnp
from jax import lax
from jax.experimental import pallas as pl
from jax.experimental.pallas import tpu as pltpu
from jax.sharding import PartitionSpec as P

BF = jnp.bfloat16
F32 = jnp.float32
I32 = jnp.int32
LANES = 128
CHIPS_Z = 8


def dot(a, b):
    return jnp.dot(a, b, preferred_element_type=F32)


def dot_t(a, b):
    return lax.dot_general(a, b, (((0,), (0,)), ((), ())), preferred_element_type=F32)


def dot_r(a, b):
    return lax.dot_general(a, b, (((1,), (1,)), ((), ())), preferred_element_type=F32)


def pack(rows, slots):
    count, width = rows.shape
    parts = [
        rows[:, i : i + LANES].reshape(count // slots, slots, LANES) for i in range(0, width, LANES)
    ]
    return jnp.concatenate(parts, axis=1).astype(BF)


def unpack(packed, slots):
    wide = packed.astype(F32)
    groups, rows, _ = wide.shape
    parts = [
        wide[:, i : i + slots, :].reshape(groups * slots, LANES) for i in range(0, rows, slots)
    ]
    return jnp.concatenate(parts, axis=1).astype(BF)


def kernel(
    dims,
    slot_of,
    used,
    feat,
    cot,
    slot_row,
    counts,
    tiles,
    ws1,
    wn1,
    ws2,
    wn2,
    out,
    gout,
    tiles_v,
    w_v,
    onehot,
    onehot_t,
    adj,
    adj_t,
    send,
    recv,
    left,
    hid_all,
    right,
    back_f32,
    rs_send,
    rs_recv,
    pre_v,
    own_v,
    acc,
    s0s,
    s0r,
    s1s,
    s1r,
    s2s,
    s2r,
    fin,
    lsem,
    esem,
    ersem,
    ysem,
    yrsem,
    gsem,
    cr_sem,
    xr_sem,
    zr_sem,
    za_sem,
    xa_sem,
    ca_sem,
):
    doms, hids, slots, masters, narrow = dims
    chips_z = CHIPS_Z
    chips_x = doms // (2 * chips_z)
    size = tiles.shape[1]
    mirrors = doms * slots
    blocks = (masters + mirrors) // size
    width = hids * narrow
    me = lax.axis_index("dom")
    hid = lax.axis_index("hid")
    core = lax.rem(me, 2)
    chip = me // 2
    cx, cz = chip // chips_z, lax.rem(chip, chips_z)

    def remote(src, dst, ssem, rsem, **where):
        return pltpu.make_async_remote_copy(
            src_ref=src,
            dst_ref=dst,
            send_sem=ssem,
            recv_sem=rsem,
            device_id=where,
            device_id_type=pl.DeviceIdType.MESH,
        )

    barrier = pltpu.get_barrier_semaphore()

    def greet(i, carry):
        pl.semaphore_signal(
            barrier,
            inc=1,
            device_id={"dom": lax.rem(me + i, doms)},
            device_id_type=pl.DeviceIdType.MESH,
        )
        return carry

    lax.fori_loop(1, doms, greet, 0)
    for i in range(1, hids):
        pl.semaphore_signal(
            barrier,
            inc=1,
            device_id={"hid": lax.rem(hid + i, hids)},
            device_id_type=pl.DeviceIdType.MESH,
        )

    loads = [pltpu.make_async_copy(tiles, tiles_v, lsem.at[0])]
    for i, w in enumerate((ws1, ws2, wn1, wn2)):
        loads.append(pltpu.make_async_copy(w, w_v.at[i], lsem.at[i + 1]))
    for load in loads:
        load.start()

    grp = lax.broadcasted_iota(I32, (doms, mirrors), 0)
    col = lax.broadcasted_iota(I32, (doms, mirrors), 1)
    repeat = (col // slots == grp).astype(F32)
    live_count = dot(jnp.broadcast_to(counts[...].astype(F32), (8, doms)), repeat)[0:1]
    lane = lax.broadcasted_iota(I32, (1, mirrors), 1)
    live = lax.rem(lane, slots).astype(F32) + 0.5 < live_count
    slot = jnp.where(live, slot_row[...], -1)
    row = lax.broadcasted_iota(I32, (masters, mirrors), 0)
    hot = (row == slot).astype(F32)
    onehot_t[...] = hot.astype(BF)
    onehot[...] = hot.T.astype(BF)

    send[0] = pack(dot(onehot[...], feat[...]), slots)
    send[1] = pack(dot(onehot[...], cot[...]), slots)
    for n in range(recv.shape[0]):
        recv[n, me] = jnp.zeros(recv.shape[2:], BF)
    left[0, hid] = feat[...]
    right[0] = cot[...]

    pl.semaphore_wait(barrier, doms - 1 + hids - 1)

    def exchange_start(n):
        def one(i, carry):
            peer = lax.rem(me + i, doms)
            remote(send.at[n, peer], recv.at[n, me], esem.at[n], ersem.at[n], dom=peer).start()
            return carry

        lax.fori_loop(1, doms, one, 0)

    def exchange_wait(n):
        some = pl.ds(0, doms - 1)
        done = remote(
            send.at[n, some], recv.at[n, some], esem.at[n], ersem.at[n], dom=lax.rem(me + 1, doms)
        )
        done.wait_recv()
        done.wait_send()
        return unpack(recv[n], slots)

    def gather_start(n, src, dst):
        for i in range(1, hids):
            remote(src, dst, ysem.at[n], yrsem.at[n], hid=lax.rem(hid + i, hids)).start()

    def gather_wait(n, src, dst):
        some = pl.ds(0, hids - 1)
        done = remote(src.at[some], dst.at[some], ysem.at[n], yrsem.at[n], hid=lax.rem(hid + 1, hids))
        done.wait_recv()
        done.wait_send()

    exchange_start(0)
    gather_start(0, feat, left.at[0, hid])
    exchange_start(1)

    loads[0].wait()
    for r in range(blocks):
        for c in range(blocks):
            e = r * blocks + c
            tile = jnp.where(used[e] > 0, tiles_v[slot_of[e]], jnp.zeros((), BF))
            rs, cs = pl.ds(r * size, size), pl.ds(c * size, size)
            adj[rs, cs] = tile
            adj_t[cs, rs] = tile.astype(F32).T.astype(BF)

    for load in loads[1:]:
        load.wait()

    def block(h):
        return pl.ds(h * narrow, narrow)

    for h in range(hids):
        back_f32[h] = dot_r(cot[...], w_v[1, block(h)])

    top, low = pl.ds(0, masters), pl.ds(masters, mirrors)
    held = exchange_wait(0)
    send[2] = pack(dot(adj[low, top], feat[...]) + dot(adj[low, low], held), slots)
    exchange_start(2)
    own_v[0] = dot(adj[top, top], feat[...]) + dot(adj[top, low], held)

    held = exchange_wait(1)
    send[3] = pack(dot(adj_t[low, top], cot[...]) + dot(adj_t[low, low], held), slots)
    exchange_start(3)
    own_v[1] = dot(adj_t[top, top], cot[...]) + dot(adj_t[top, low], held)

    gather_wait(0, left.at[0], left.at[0])
    pre = dot(left[0, 0], w_v[0, block(0)])
    for h in range(1, hids):
        pre += dot(left[0, h], w_v[0, block(h)])
    pre_v[...] = pre

    left[1, hid] = (own_v[0] + dot(onehot_t[...], exchange_wait(2))).astype(BF)
    gather_start(1, left.at[1, hid], left.at[1, hid])
    right[1] = (own_v[1] + dot(onehot_t[...], exchange_wait(3))).astype(BF)
    for h in range(hids):
        rs_send[h] = (back_f32[h] + dot_r(right[1], w_v[3, block(h)])).astype(BF)
    for i in range(1, hids):
        peer = lax.rem(hid + i, hids)
        remote(rs_send.at[peer], rs_recv.at[hid], ysem.at[2], yrsem.at[2], hid=peer).start()

    gather_wait(1, left.at[1], left.at[1])
    pre = pre_v[...]
    for h in range(hids):
        pre += dot(left[1, h], w_v[2, block(h)])
    sigma = jax.nn.sigmoid(pre)
    hid_all[hid] = (pre * sigma).astype(BF)
    gather_start(3, hid_all.at[hid], hid_all.at[hid])

    gather_wait(2, rs_send, rs_recv)
    back_one = rs_send[hid].astype(F32)
    for i in range(1, hids):
        back_one += rs_recv[lax.rem(hid + i, hids)].astype(F32)
    back_pre = (back_one * sigma * (1.0 + pre * (1.0 - sigma))).astype(BF)

    sibling = me + 1 - 2 * core
    piece = width // chips_x
    chunk = piece // chips_z
    factor = 1.0 / math.sqrt(doms * masters)
    z_order = sorted(range(chips_z), key=lambda j: -min(j, chips_z - j))

    def dom_of(x, z):
        return (x * chips_z + z) * 2 + core

    def to_sibling(g):
        return remote(s0s.at[g], s0r.at[g], gsem.at[g, 0], cr_sem.at[g], dom=sibling)

    def x_start(g):
        done = to_sibling(g)
        done.wait_recv()
        done.wait_send()
        s1s[g] = (acc[g] + s0r[g].astype(F32)).astype(BF)
        for j in z_order:
            rows = lax.rem(cz + j, chips_z) * chunk
            for i in range(1, chips_x):
                px = lax.rem(cx + i, chips_x)
                remote(
                    s1s.at[g, pl.ds(px * piece + rows, chunk)],
                    s1r.at[g, j, cx],
                    gsem.at[g, 1],
                    xr_sem.at[g, j],
                    dom=dom_of(px, cz),
                ).start()

    def z_start(g):
        for j in z_order:
            pz = lax.rem(cz + j, chips_z)
            some = s1r.at[g, j, pl.ds(0, chips_x - 1)]
            remote(some, some, gsem.at[g, 1], xr_sem.at[g, j], dom=sibling).wait_recv()
            mine = pl.ds(cx * piece + pz * chunk, chunk)
            total = acc[g, mine] + s0r[g, mine].astype(F32)
            for i in range(1, chips_x):
                total += s1r[g, j, lax.rem(cx + i, chips_x)].astype(F32)
            if j == 0:
                acc[g, mine] = total
                continue
            s2s[g, j] = total.astype(BF)
            remote(
                s2s.at[g, j], s2r.at[g, cz], gsem.at[g, 2], zr_sem.at[g], dom=dom_of(cx, pz)
            ).start()

    def chunk_at(g, x, z):
        return gout.at[g, core, pl.ds(x * piece + z * chunk, chunk)]

    def finish(g):
        some = s2r.at[g, pl.ds(0, chips_z - 1)]
        remote(some, some, gsem.at[g, 2], zr_sem.at[g], dom=sibling).wait_recv()
        total = acc[g, pl.ds(cx * piece + cz * chunk, chunk)]
        for i in range(1, chips_z):
            total += s2r[g, lax.rem(cz + i, chips_z)].astype(F32)
        fin[g] = (total * factor).astype(BF)
        place = chunk_at(g, cx, cz)
        for j in z_order:
            if j:
                pz = lax.rem(cz + j, chips_z)
                remote(fin.at[g], place, gsem.at[g, 3], za_sem.at[g, j], dom=dom_of(cx, pz)).start()
        for i in range(1, chips_x):
            px = lax.rem(cx + i, chips_x)
            remote(fin.at[g], place, gsem.at[g, 4], xa_sem.at[g], dom=dom_of(px, cz)).start()
        pltpu.make_async_copy(fin.at[g], place, lsem.at[5 + g]).start()

    def forward(g):
        for j in reversed(z_order):
            if j:
                place = chunk_at(g, cx, lax.rem(cz + chips_z - j, chips_z))
                remote(place, place, gsem.at[g, 3], za_sem.at[g, j], dom=sibling).wait_recv()
                for i in range(1, chips_x):
                    px = lax.rem(cx + i, chips_x)
                    remote(place, place, gsem.at[g, 4], xa_sem.at[g], dom=dom_of(px, cz)).start()

    def core_back(g):
        place = chunk_at(g, cx, cz)
        pltpu.make_async_copy(fin.at[g], place, lsem.at[5 + g]).wait()
        some = gout.at[g, core, pl.ds(0, (chips_x - 1) * piece)]
        remote(some, some, gsem.at[g, 4], xa_sem.at[g], dom=sibling).wait_recv()
        mine = gout.at[g, core]
        remote(mine, mine, gsem.at[g, 5], ca_sem.at[g], dom=sibling).start()

    def drain(g):
        def sent(stage, ref):
            remote(ref, ref, gsem.at[g, stage], ca_sem.at[g], dom=sibling).wait_send()

        most = (chips_x - 1) * piece
        sent(1, s1s.at[g, pl.ds(0, most)])
        sent(2, s2s.at[g, pl.ds(0, chips_z - 1)])
        sent(3, s2s.at[g, pl.ds(0, chips_z - 1)])
        sent(4, s1s.at[g, pl.ds(0, most)])
        mine = gout.at[g, core]
        done = remote(mine, mine, gsem.at[g, 5], ca_sem.at[g], dom=sibling)
        done.wait_recv()
        done.wait_send()

    for h in range(hids):
        s0s[0, block(h)] = dot_t(left[1 - core, h], back_pre).astype(BF)
    to_sibling(0).start()
    for h in range(hids):
        acc[0, block(h)] = dot_t(left[core, h], back_pre)
    x_start(0)

    gather_wait(3, hid_all, hid_all)
    mixed = dot(hid_all[0], w_v[3, block(0)])
    for h in range(1, hids):
        mixed += dot(hid_all[h], w_v[3, block(h)])
    mixed = mixed.astype(BF)
    send[4] = pack(dot(onehot[...], mixed), slots)
    exchange_start(4)

    for h in range(hids):
        s0s[1, block(h)] = dot_t(hid_all[h], right[1 - core]).astype(BF)
    to_sibling(1).start()
    for h in range(hids):
        acc[1, block(h)] = dot_t(hid_all[h], right[core])
    x_start(1)
    z_start(0)
    finish(0)

    held = exchange_wait(4)
    send[5] = pack(dot(adj[low, top], mixed) + dot(adj[low, low], held), slots)
    exchange_start(5)
    z_start(1)
    forward(0)
    total = dot(adj[top, top], mixed) + dot(adj[top, low], held)
    for h in range(hids):
        total += dot(hid_all[h], w_v[1, block(h)])
    own_v[0] = total
    finish(1)
    core_back(0)
    forward(1)
    out[...] = (own_v[0] + dot(onehot_t[...], exchange_wait(5))).astype(BF)
    core_back(1)
    drain(0)
    drain(1)


def local(
    feat,
    cotangent,
    tiles,
    tile_index,
    tile_count,
    replica_slot,
    recv_count,
    w_self1,
    w_neigh1,
    w_self2,
    w_neigh2,
):
    doms, hids = lax.axis_size("dom"), lax.axis_size("hid")
    masters, narrow = feat.shape
    width = narrow * hids
    mirrors = replica_slot.shape[1]
    slots = mirrors // doms
    size = tiles.shape[2]
    blocks = (masters + mirrors) // size
    side = blocks * size
    chips_x = doms // (2 * CHIPS_Z)
    piece = width // chips_x
    chunk = piece // CHIPS_Z

    order = jnp.arange(tiles.shape[1], dtype=I32)
    match = (
        (tile_index[0][None, :] == jnp.arange(blocks * blocks, dtype=I32)[:, None])
        & (order < tile_count[0])[None, :]
    ).astype(I32)
    slot_of = (match * order[None, :]).sum(axis=1)
    used = match.sum(axis=1)

    packed = slots * narrow // LANES
    smem = pl.BlockSpec(memory_space=pltpu.SMEM)
    vmem = pl.BlockSpec(memory_space=pltpu.VMEM)
    anym = pl.BlockSpec(memory_space=pl.ANY)
    dma = pltpu.SemaphoreType.DMA

    def body(*refs):
        kernel((doms, hids, slots, masters, narrow), *refs)

    out, grads = pl.pallas_call(
        body,
        out_shape=(
            jax.ShapeDtypeStruct((masters, narrow), BF),
            jax.ShapeDtypeStruct((2, 2, width, narrow), BF),
        ),
        in_specs=[smem] * 2 + [vmem] * 4 + [anym] * 5,
        out_specs=(vmem, anym),
        scratch_shapes=[
            pltpu.VMEM(tiles.shape[1:], BF),
            pltpu.VMEM((4, width, narrow), BF),
            pltpu.VMEM((mirrors, masters), BF),
            pltpu.VMEM((masters, mirrors), BF),
            pltpu.VMEM((side, side), BF),
            pltpu.VMEM((side, side), BF),
            pltpu.VMEM((6, doms, packed, LANES), BF),
            pltpu.VMEM((6, doms, packed, LANES), BF),
            pltpu.VMEM((2, hids, masters, narrow), BF),
            pltpu.VMEM((hids, masters, narrow), BF),
            pltpu.VMEM((2, masters, narrow), BF),
            pltpu.VMEM((hids, masters, narrow), F32),
            pltpu.VMEM((hids, masters, narrow), BF),
            pltpu.VMEM((hids, masters, narrow), BF),
            pltpu.VMEM((masters, narrow), F32),
            pltpu.VMEM((2, masters, narrow), F32),
            pltpu.VMEM((2, width, narrow), F32),
            pltpu.VMEM((2, width, narrow), BF),
            pltpu.VMEM((2, width, narrow), BF),
            pltpu.VMEM((2, width, narrow), BF),
            pltpu.VMEM((2, CHIPS_Z, chips_x, chunk, narrow), BF),
            pltpu.VMEM((2, CHIPS_Z, chunk, narrow), BF),
            pltpu.VMEM((2, CHIPS_Z, chunk, narrow), BF),
            pltpu.VMEM((2, chunk, narrow), BF),
            dma((7,)),
            dma((6,)),
            dma((6,)),
            dma((4,)),
            dma((4,)),
            dma((2, 6)),
            dma((2,)),
            dma((2, CHIPS_Z)),
            dma((2,)),
            dma((2, CHIPS_Z)),
            dma((2,)),
            dma((2,)),
        ],
        compiler_params=pltpu.CompilerParams(
            collective_id=0, has_side_effects=True, vmem_limit_bytes=60 * 1024 * 1024
        ),
    )(
        slot_of,
        used,
        feat,
        cotangent,
        replica_slot,
        recv_count,
        tiles[0],
        w_self1,
        w_neigh1,
        w_self2,
        w_neigh2,
    )
    grads = grads.astype(F32)
    return (out, grads[0, 0], grads[0, 1], grads[1, 0], grads[1, 1])


def solution(mesh):
    rows = P("dom", "hid")
    cols = P(None, "hid")
    return jax.shard_map(
        local,
        mesh=mesh,
        in_specs=(
            rows,
            rows,
            P("dom", None, None, None),
            P("dom", None),
            P("dom"),
            P("dom", None),
            P("dom", None),
            cols,
            cols,
            cols,
            cols,
        ),
        out_specs=(rows, cols, cols, cols, cols),
        check_vma=False,
    )
```

```python
import math

import jax
import jax.numpy as jnp
from jax import lax
from jax.experimental import pallas as pl
from jax.experimental.pallas import tpu as pltpu
from jax.sharding import PartitionSpec as P

BF = jnp.bfloat16
F32 = jnp.float32
I32 = jnp.int32
LANES = 128
CHIPS_Z = 8


def dot(a, b):
    return jnp.dot(a, b, preferred_element_type=F32)


def dot_t(a, b):
    return lax.dot_general(a, b, (((0,), (0,)), ((), ())), preferred_element_type=F32)


def dot_r(a, b):
    return lax.dot_general(a, b, (((1,), (1,)), ((), ())), preferred_element_type=F32)


def pack(rows, slots):
    count, width = rows.shape
    parts = [
        rows[:, i : i + LANES].reshape(count // slots, slots, LANES) for i in range(0, width, LANES)
    ]
    return jnp.concatenate(parts, axis=1).astype(BF)


def unpack(packed, slots):
    wide = packed.astype(F32)
    groups, rows, _ = wide.shape
    parts = [
        wide[:, i : i + slots, :].reshape(groups * slots, LANES) for i in range(0, rows, slots)
    ]
    return jnp.concatenate(parts, axis=1).astype(BF)


def kernel(
    dims,
    tile_at,
    tile_total,
    feat,
    cot,
    slot_row,
    counts,
    tiles,
    ws1,
    wn1,
    ws2,
    wn2,
    out,
    gout,
    tiles_v,
    w_v,
    onehot,
    onehot_t,
    adj,
    adj_t,
    send,
    recv,
    left,
    hid_all,
    right,
    rs_send,
    rs_recv,
    pre_v,
    own_v,
    acc,
    s0s,
    s0r,
    s1s,
    s1r,
    s2s,
    s2r,
    fin,
    lsem,
    esem,
    ersem,
    ysem,
    yrsem,
    gsem,
    cr_sem,
    xr_sem,
    zr_sem,
    za_sem,
    xa_sem,
    ca_sem,
):
    doms, hids, slots, masters, narrow = dims
    chips_z = CHIPS_Z
    chips_x = doms // (2 * chips_z)
    size = tiles.shape[1]
    mirrors = doms * slots
    blocks = (masters + mirrors) // size
    width = hids * narrow
    me = lax.axis_index("dom")
    hid = lax.axis_index("hid")
    core = lax.rem(me, 2)
    chip = me // 2
    cx, cz = chip // chips_z, lax.rem(chip, chips_z)

    def remote(src, dst, ssem, rsem, **where):
        return pltpu.make_async_remote_copy(
            src_ref=src,
            dst_ref=dst,
            send_sem=ssem,
            recv_sem=rsem,
            device_id=where,
            device_id_type=pl.DeviceIdType.MESH,
        )

    barrier = pltpu.get_barrier_semaphore()

    def greet(i, carry):
        pl.semaphore_signal(
            barrier,
            inc=1,
            device_id={"dom": lax.rem(me + i, doms)},
            device_id_type=pl.DeviceIdType.MESH,
        )
        return carry

    lax.fori_loop(1, doms, greet, 0)
    for i in range(1, hids):
        pl.semaphore_signal(
            barrier,
            inc=1,
            device_id={"hid": lax.rem(hid + i, hids)},
            device_id_type=pl.DeviceIdType.MESH,
        )

    loads = [pltpu.make_async_copy(tiles, tiles_v, lsem.at[0])]
    for i, w in enumerate((ws1, ws2, wn1, wn2)):
        loads.append(pltpu.make_async_copy(w, w_v.at[i], lsem.at[i + 1]))
    for i in (4, 0, 2, 1, 3):
        loads[i].start()

    grp = lax.broadcasted_iota(I32, (doms, mirrors), 0)
    col = lax.broadcasted_iota(I32, (doms, mirrors), 1)
    repeat = (col // slots == grp).astype(F32)
    live_count = dot(jnp.broadcast_to(counts[...].astype(F32), (8, doms)), repeat)[0:1]
    lane = lax.broadcasted_iota(I32, (1, mirrors), 1)
    live = lax.rem(lane, slots).astype(F32) + 0.5 < live_count
    slot = jnp.where(live, slot_row[...], -1)
    row = lax.broadcasted_iota(I32, (masters, mirrors), 0)
    hot = (row == slot).astype(F32)
    onehot_t[...] = hot.astype(BF)
    onehot[...] = hot.T.astype(BF)

    send[0] = pack(dot(onehot[...], feat[...]), slots)
    for n in range(recv.shape[0]):
        recv[n, me] = jnp.zeros(recv.shape[2:], BF)

    pl.semaphore_wait(barrier, doms - 1 + hids - 1)

    def exchange_start(n):
        def one(i, carry):
            peer = lax.rem(me + i, doms)
            remote(send.at[n, peer], recv.at[n, me], esem.at[n], ersem.at[n], dom=peer).start()
            return carry

        lax.fori_loop(1, doms, one, 0)

    def exchange_wait(n):
        some = pl.ds(0, doms - 1)
        done = remote(
            send.at[n, some], recv.at[n, some], esem.at[n], ersem.at[n], dom=lax.rem(me + 1, doms)
        )
        done.wait_recv()
        done.wait_send()
        return unpack(recv[n], slots)

    def gather_start(n, src, dst):
        for i in range(1, hids):
            remote(src, dst, ysem.at[n], yrsem.at[n], hid=lax.rem(hid + i, hids)).start()

    def gather_wait(n, src, dst):
        some = pl.ds(0, hids - 1)
        done = remote(src.at[some], dst.at[some], ysem.at[n], yrsem.at[n], hid=lax.rem(hid + 1, hids))
        done.wait_recv()
        done.wait_send()

    def scatter_start(n):
        for i in range(1, hids):
            peer = lax.rem(hid + i, hids)
            remote(
                rs_send.at[n, peer], rs_recv.at[n, hid], ysem.at[2 + n], yrsem.at[2 + n], hid=peer
            ).start()

    def scatter_wait(n):
        gather_wait(2 + n, rs_send.at[n], rs_recv.at[n])
        total = rs_send[n, hid].astype(F32)
        for i in range(1, hids):
            total += rs_recv[n, lax.rem(hid + i, hids)].astype(F32)
        return total

    def block(h):
        return pl.ds(h * narrow, narrow)

    exchange_start(0)
    loads[4].wait()
    for h in range(hids):
        rs_send[0, h] = dot_r(cot[...], w_v[3, block(h)]).astype(BF)
    scatter_start(0)
    gather_start(0, feat, left.at[0, hid])
    send[1] = pack(dot(onehot[...], cot[...]), slots)
    exchange_start(1)
    left[0, hid] = feat[...]
    right[0] = cot[...]

    loads[0].wait()
    total_tiles = tile_total[0]
    for r in range(blocks):
        for c in range(blocks):
            e = r * blocks + c
            found = jnp.int32(0)
            for t in range(tiles.shape[0]):
                hit = jnp.logical_and(tile_at[0, t] == e, t < total_tiles)
                found = jnp.where(hit, t + 1, found)
            tile = jnp.where(found > 0, tiles_v[jnp.maximum(found - 1, 0)], jnp.zeros((), BF))
            rs, cs = pl.ds(r * size, size), pl.ds(c * size, size)
            adj[rs, cs] = tile
            adj_t[cs, rs] = tile.astype(F32).T.astype(BF)

    loads[2].wait()
    for h in range(hids):
        rs_send[1, h] = dot_r(cot[...], w_v[1, block(h)]).astype(BF)
    scatter_start(1)

    top, low = pl.ds(0, masters), pl.ds(masters, mirrors)
    held = exchange_wait(0)
    send[2] = pack(dot(adj[low, top], feat[...]) + dot(adj[low, low], held), slots)
    exchange_start(2)
    own_v[0] = dot(adj[top, top], feat[...]) + dot(adj[top, low], held)

    back_agg = scatter_wait(0).astype(BF)
    send[3] = pack(dot(onehot[...], back_agg), slots)
    exchange_start(3)

    held = exchange_wait(1)
    send[5] = pack(dot(adj_t[low, top], cot[...]) + dot(adj_t[low, low], held), slots)
    own_v[1] = dot(adj_t[top, top], cot[...]) + dot(adj_t[top, low], held)

    gather_wait(0, left.at[0], left.at[0])
    loads[1].wait()
    loads[3].wait()
    pre = dot(left[0, 0], w_v[0, block(0)])
    for h in range(1, hids):
        pre += dot(left[0, h], w_v[0, block(h)])
    pre_v[...] = pre

    left[1, hid] = (own_v[0] + dot(onehot_t[...], exchange_wait(2))).astype(BF)
    gather_start(1, left.at[1, hid], left.at[1, hid])

    held = exchange_wait(3)
    send[4] = pack(dot(adj_t[low, top], back_agg) + dot(adj_t[low, low], held), slots)
    exchange_start(4)
    exchange_start(5)
    own_v[0] = (
        dot(adj_t[top, top], back_agg) + dot(adj_t[top, low], held) + scatter_wait(1)
    )

    gather_wait(1, left.at[1], left.at[1])
    pre = pre_v[...]
    for h in range(hids):
        pre += dot(left[1, h], w_v[2, block(h)])
    sigma = jax.nn.sigmoid(pre)
    hid_all[hid] = (pre * sigma).astype(BF)
    gather_start(4, hid_all.at[hid], hid_all.at[hid])

    back_one = own_v[0] + dot(onehot_t[...], exchange_wait(4))
    back_pre = (back_one * sigma * (1.0 + pre * (1.0 - sigma))).astype(BF)

    sibling = me + 1 - 2 * core
    piece = width // chips_x
    chunk = piece // chips_z
    factor = 1.0 / math.sqrt(doms * masters)
    z_order = sorted(range(chips_z), key=lambda j: -min(j, chips_z - j))

    def dom_of(x, z):
        return (x * chips_z + z) * 2 + core

    def to_sibling(g):
        return remote(s0s.at[g], s0r.at[g], gsem.at[g, 0], cr_sem.at[g], dom=sibling)

    def x_start(g):
        done = to_sibling(g)
        done.wait_recv()
        done.wait_send()
        s1s[g] = (acc[g] + s0r[g].astype(F32)).astype(BF)
        for j in z_order:
            rows = lax.rem(cz + j, chips_z) * chunk
            for i in range(1, chips_x):
                px = lax.rem(cx + i, chips_x)
                remote(
                    s1s.at[g, pl.ds(px * piece + rows, chunk)],
                    s1r.at[g, j, cx],
                    gsem.at[g, 1],
                    xr_sem.at[g, j],
                    dom=dom_of(px, cz),
                ).start()

    def z_start(g):
        for j in z_order:
            pz = lax.rem(cz + j, chips_z)
            some = s1r.at[g, j, pl.ds(0, chips_x - 1)]
            remote(some, some, gsem.at[g, 1], xr_sem.at[g, j], dom=sibling).wait_recv()
            mine = pl.ds(cx * piece + pz * chunk, chunk)
            total = acc[g, mine] + s0r[g, mine].astype(F32)
            for i in range(1, chips_x):
                total += s1r[g, j, lax.rem(cx + i, chips_x)].astype(F32)
            if j == 0:
                acc[g, mine] = total
                continue
            s2s[g, j] = total.astype(BF)
            remote(
                s2s.at[g, j], s2r.at[g, cz], gsem.at[g, 2], zr_sem.at[g], dom=dom_of(cx, pz)
            ).start()

    def chunk_at(g, x, z):
        return gout.at[g, core, pl.ds(x * piece + z * chunk, chunk)]

    def finish(g):
        some = s2r.at[g, pl.ds(0, chips_z - 1)]
        remote(some, some, gsem.at[g, 2], zr_sem.at[g], dom=sibling).wait_recv()
        total = acc[g, pl.ds(cx * piece + cz * chunk, chunk)]
        for i in range(1, chips_z):
            total += s2r[g, lax.rem(cz + i, chips_z)].astype(F32)
        fin[g] = (total * factor).astype(BF)
        place = chunk_at(g, cx, cz)
        for j in z_order:
            if j:
                pz = lax.rem(cz + j, chips_z)
                remote(fin.at[g], place, gsem.at[g, 3], za_sem.at[g, j], dom=dom_of(cx, pz)).start()
        for i in range(1, chips_x):
            px = lax.rem(cx + i, chips_x)
            remote(fin.at[g], place, gsem.at[g, 4], xa_sem.at[g], dom=dom_of(px, cz)).start()
        pltpu.make_async_copy(fin.at[g], place, lsem.at[5 + g]).start()

    def forward(g):
        for j in reversed(z_order):
            if j:
                place = chunk_at(g, cx, lax.rem(cz + chips_z - j, chips_z))
                remote(place, place, gsem.at[g, 3], za_sem.at[g, j], dom=sibling).wait_recv()
                for i in range(1, chips_x):
                    px = lax.rem(cx + i, chips_x)
                    remote(place, place, gsem.at[g, 4], xa_sem.at[g], dom=dom_of(px, cz)).start()

    def core_back(g):
        place = chunk_at(g, cx, cz)
        pltpu.make_async_copy(fin.at[g], place, lsem.at[5 + g]).wait()
        some = gout.at[g, core, pl.ds(0, (chips_x - 1) * piece)]
        remote(some, some, gsem.at[g, 4], xa_sem.at[g], dom=sibling).wait_recv()
        mine = gout.at[g, core]
        remote(mine, mine, gsem.at[g, 5], ca_sem.at[g], dom=sibling).start()

    def drain(g):
        def sent(stage, ref):
            remote(ref, ref, gsem.at[g, stage], ca_sem.at[g], dom=sibling).wait_send()

        most = (chips_x - 1) * piece
        sent(1, s1s.at[g, pl.ds(0, most)])
        sent(2, s2s.at[g, pl.ds(0, chips_z - 1)])
        sent(3, s2s.at[g, pl.ds(0, chips_z - 1)])
        sent(4, s1s.at[g, pl.ds(0, most)])
        mine = gout.at[g, core]
        done = remote(mine, mine, gsem.at[g, 5], ca_sem.at[g], dom=sibling)
        done.wait_recv()
        done.wait_send()

    for h in range(hids):
        s0s[0, block(h)] = dot_t(left[1 - core, h], back_pre).astype(BF)
    to_sibling(0).start()
    for h in range(hids):
        acc[0, block(h)] = dot_t(left[core, h], back_pre)
    x_start(0)

    right[1] = (own_v[1] + dot(onehot_t[...], exchange_wait(5))).astype(BF)
    gather_wait(4, hid_all, hid_all)
    mixed = dot(hid_all[0], w_v[3, block(0)])
    for h in range(1, hids):
        mixed += dot(hid_all[h], w_v[3, block(h)])
    mixed = mixed.astype(BF)
    send[6] = pack(dot(onehot[...], mixed), slots)
    exchange_start(6)

    for h in range(hids):
        s0s[1, block(h)] = dot_t(hid_all[h], right[1 - core]).astype(BF)
    to_sibling(1).start()
    for h in range(hids):
        acc[1, block(h)] = dot_t(hid_all[h], right[core])
    x_start(1)
    z_start(0)
    finish(0)

    held = exchange_wait(6)
    send[7] = pack(dot(adj[low, top], mixed) + dot(adj[low, low], held), slots)
    exchange_start(7)
    z_start(1)
    forward(0)
    total = dot(adj[top, top], mixed) + dot(adj[top, low], held)
    for h in range(hids):
        total += dot(hid_all[h], w_v[1, block(h)])
    own_v[0] = total
    finish(1)
    core_back(0)
    forward(1)
    out[...] = (own_v[0] + dot(onehot_t[...], exchange_wait(7))).astype(BF)
    core_back(1)
    drain(0)
    drain(1)


def local(
    feat,
    cotangent,
    tiles,
    tile_index,
    tile_count,
    replica_slot,
    recv_count,
    w_self1,
    w_neigh1,
    w_self2,
    w_neigh2,
):
    doms, hids = lax.axis_size("dom"), lax.axis_size("hid")
    masters, narrow = feat.shape
    width = narrow * hids
    mirrors = replica_slot.shape[1]
    slots = mirrors // doms
    size = tiles.shape[2]
    blocks = (masters + mirrors) // size
    side = blocks * size
    chips_x = doms // (2 * CHIPS_Z)
    piece = width // chips_x
    chunk = piece // CHIPS_Z

    packed = slots * narrow // LANES
    smem = pl.BlockSpec(memory_space=pltpu.SMEM)
    vmem = pl.BlockSpec(memory_space=pltpu.VMEM)
    anym = pl.BlockSpec(memory_space=pl.ANY)
    dma = pltpu.SemaphoreType.DMA

    def body(*refs):
        kernel((doms, hids, slots, masters, narrow), *refs)

    out, grads = pl.pallas_call(
        body,
        out_shape=(
            jax.ShapeDtypeStruct((masters, narrow), BF),
            jax.ShapeDtypeStruct((2, 2, width, narrow), BF),
        ),
        in_specs=[smem] * 2 + [vmem] * 4 + [anym] * 5,
        out_specs=(vmem, anym),
        scratch_shapes=[
            pltpu.VMEM(tiles.shape[1:], BF),
            pltpu.VMEM((4, width, narrow), BF),
            pltpu.VMEM((mirrors, masters), BF),
            pltpu.VMEM((masters, mirrors), BF),
            pltpu.VMEM((side, side), BF),
            pltpu.VMEM((side, side), BF),
            pltpu.VMEM((8, doms, packed, LANES), BF),
            pltpu.VMEM((8, doms, packed, LANES), BF),
            pltpu.VMEM((2, hids, masters, narrow), BF),
            pltpu.VMEM((hids, masters, narrow), BF),
            pltpu.VMEM((2, masters, narrow), BF),
            pltpu.VMEM((2, hids, masters, narrow), BF),
            pltpu.VMEM((2, hids, masters, narrow), BF),
            pltpu.VMEM((masters, narrow), F32),
            pltpu.VMEM((2, masters, narrow), F32),
            pltpu.VMEM((2, width, narrow), F32),
            pltpu.VMEM((2, width, narrow), BF),
            pltpu.VMEM((2, width, narrow), BF),
            pltpu.VMEM((2, width, narrow), BF),
            pltpu.VMEM((2, CHIPS_Z, chips_x, chunk, narrow), BF),
            pltpu.VMEM((2, CHIPS_Z, chunk, narrow), BF),
            pltpu.VMEM((2, CHIPS_Z, chunk, narrow), BF),
            pltpu.VMEM((2, chunk, narrow), BF),
            dma((7,)),
            dma((8,)),
            dma((8,)),
            dma((5,)),
            dma((5,)),
            dma((2, 6)),
            dma((2,)),
            dma((2, CHIPS_Z)),
            dma((2,)),
            dma((2, CHIPS_Z)),
            dma((2,)),
            dma((2,)),
        ],
        compiler_params=pltpu.CompilerParams(
            collective_id=0, has_side_effects=True, vmem_limit_bytes=60 * 1024 * 1024
        ),
    )(
        tile_index,
        tile_count,
        feat,
        cotangent,
        replica_slot,
        recv_count,
        tiles[0],
        w_self1,
        w_neigh1,
        w_self2,
        w_neigh2,
    )
    return (out, *(grads[i // 2, i % 2].astype(F32) for i in range(4)))


def solution(mesh):
    rows = P("dom", "hid")
    cols = P(None, "hid")
    return jax.shard_map(
        local,
        mesh=mesh,
        in_specs=(
            rows,
            rows,
            P("dom", None, None, None),
            P("dom", None),
            P("dom"),
            P("dom", None),
            P("dom", None),
            cols,
            cols,
            cols,
            cols,
        ),
        out_specs=(rows, cols, cols, cols, cols),
        check_vma=False,
    )
```

```python
import math

import jax
import jax.numpy as jnp
from jax import lax
from jax.experimental import pallas as pl
from jax.experimental.pallas import tpu as pltpu
from jax.sharding import PartitionSpec as P

BF = jnp.bfloat16
F32 = jnp.float32
I32 = jnp.int32
LANES = 128
CHIPS_Z = 8


def dot(a, b):
    return jnp.dot(a, b, preferred_element_type=F32)


def dot_t(a, b):
    return lax.dot_general(a, b, (((0,), (0,)), ((), ())), preferred_element_type=F32)


def dot_r(a, b):
    return lax.dot_general(a, b, (((1,), (1,)), ((), ())), preferred_element_type=F32)


def pack(rows, slots):
    count, width = rows.shape
    parts = [
        rows[:, i : i + LANES].reshape(count // slots, slots, LANES) for i in range(0, width, LANES)
    ]
    return jnp.concatenate(parts, axis=1).astype(BF)


def unpack(packed, slots):
    wide = packed.astype(F32)
    groups, rows, _ = wide.shape
    parts = [
        wide[:, i : i + slots, :].reshape(groups * slots, LANES) for i in range(0, rows, slots)
    ]
    return jnp.concatenate(parts, axis=1).astype(BF)


def kernel(
    dims,
    tile_at,
    tile_total,
    feat,
    cot,
    slot_row,
    counts,
    tiles,
    ws1,
    wn1,
    ws2,
    wn2,
    out,
    gout,
    tiles_v,
    w_v,
    onehot,
    onehot_t,
    adj,
    adj_t,
    send,
    recv,
    left,
    hid_all,
    agg_two,
    right,
    back_f32,
    rs_send,
    rs_recv,
    pre_v,
    own_v,
    acc,
    s0s,
    s0r,
    s1s,
    s1r,
    s2s,
    s2r,
    fin,
    lsem,
    esem,
    ersem,
    ysem,
    yrsem,
    gsem,
    cr_sem,
    xr_sem,
    zr_sem,
    za_sem,
    xa_sem,
    ca_sem,
):
    doms, hids, slots, masters, narrow = dims
    chips_z = CHIPS_Z
    chips_x = doms // (2 * chips_z)
    size = tiles.shape[1]
    mirrors = doms * slots
    blocks = (masters + mirrors) // size
    width = hids * narrow
    me = lax.axis_index("dom")
    hid = lax.axis_index("hid")
    core = lax.rem(me, 2)
    chip = me // 2
    cx, cz = chip // chips_z, lax.rem(chip, chips_z)

    def remote(src, dst, ssem, rsem, **where):
        return pltpu.make_async_remote_copy(
            src_ref=src,
            dst_ref=dst,
            send_sem=ssem,
            recv_sem=rsem,
            device_id=where,
            device_id_type=pl.DeviceIdType.MESH,
        )

    barrier = pltpu.get_barrier_semaphore()

    def greet(i, carry):
        pl.semaphore_signal(
            barrier,
            inc=1,
            device_id={"dom": lax.rem(me + i, doms)},
            device_id_type=pl.DeviceIdType.MESH,
        )
        return carry

    lax.fori_loop(1, doms, greet, 0)
    for i in range(1, hids):
        pl.semaphore_signal(
            barrier,
            inc=1,
            device_id={"hid": lax.rem(hid + i, hids)},
            device_id_type=pl.DeviceIdType.MESH,
        )

    mine_in = left.at[0, hid]
    loads = [
        pltpu.make_async_copy(src, dst, lsem.at[i])
        for i, (src, dst) in enumerate(
            (
                (feat, mine_in),
                (cot, right.at[0]),
                (tiles, tiles_v),
                (ws2, w_v.at[1]),
                (ws1, w_v.at[0]),
                (wn1, w_v.at[2]),
                (wn2, w_v.at[3]),
            )
        )
    ]
    for load in loads:
        load.start()

    grp = lax.broadcasted_iota(I32, (doms, mirrors), 0)
    col = lax.broadcasted_iota(I32, (doms, mirrors), 1)
    repeat = (col // slots == grp).astype(F32)
    live_count = dot(jnp.broadcast_to(counts[...].astype(F32), (8, doms)), repeat)[0:1]
    lane = lax.broadcasted_iota(I32, (1, mirrors), 1)
    live = lax.rem(lane, slots).astype(F32) + 0.5 < live_count
    slot = jnp.where(live, slot_row[...], -1)
    row = lax.broadcasted_iota(I32, (masters, mirrors), 0)
    hot = (row == slot).astype(F32)
    onehot_t[...] = hot.astype(BF)
    onehot[...] = hot.T.astype(BF)

    loads[0].wait()
    send[0] = pack(dot(onehot[...], mine_in[...]), slots)
    for n in range(recv.shape[0]):
        recv[n, me] = jnp.zeros(recv.shape[2:], BF)

    pl.semaphore_wait(barrier, doms - 1 + hids - 1)

    def exchange_start(n):
        def one(i, carry):
            peer = lax.rem(me + i, doms)
            remote(send.at[n, peer], recv.at[n, me], esem.at[n], ersem.at[n], dom=peer).start()
            return carry

        lax.fori_loop(1, doms, one, 0)

    def exchange_wait(n):
        some = pl.ds(0, doms - 1)
        done = remote(
            send.at[n, some], recv.at[n, some], esem.at[n], ersem.at[n], dom=lax.rem(me + 1, doms)
        )
        done.wait_recv()
        done.wait_send()
        return unpack(recv[n], slots)

    def gather_start(n, src, dst):
        for i in range(1, hids):
            remote(src, dst, ysem.at[n], yrsem.at[n], hid=lax.rem(hid + i, hids)).start()

    def gather_wait(n, src, dst):
        some = pl.ds(0, hids - 1)
        done = remote(src.at[some], dst.at[some], ysem.at[n], yrsem.at[n], hid=lax.rem(hid + 1, hids))
        done.wait_recv()
        done.wait_send()

    exchange_start(0)
    loads[1].wait()
    send[1] = pack(dot(onehot[...], right[0]), slots)
    exchange_start(1)
    gather_start(0, mine_in, mine_in)

    loads[2].wait()
    total_tiles = tile_total[0]
    for r in range(blocks):
        for c in range(blocks):
            e = r * blocks + c
            found = jnp.int32(0)
            for t in range(tiles.shape[0]):
                hit = jnp.logical_and(tile_at[0, t] == e, t < total_tiles)
                found = jnp.where(hit, t + 1, found)
            tile = jnp.where(found > 0, tiles_v[jnp.maximum(found - 1, 0)], jnp.zeros((), BF))
            rs, cs = pl.ds(r * size, size), pl.ds(c * size, size)
            adj[rs, cs] = tile
            adj_t[cs, rs] = tile.astype(F32).T.astype(BF)

    for load in loads[3:]:
        load.wait()

    def block(h):
        return pl.ds(h * narrow, narrow)

    for h in range(hids):
        back_f32[h] = dot_r(right[0], w_v[1, block(h)])

    top, low = pl.ds(0, masters), pl.ds(masters, mirrors)
    held = exchange_wait(0)
    send[2] = pack(dot(adj[low, top], mine_in[...]) + dot(adj[low, low], held), slots)
    exchange_start(2)
    own_v[0] = dot(adj[top, top], mine_in[...]) + dot(adj[top, low], held)

    held = exchange_wait(1)
    send[3] = pack(dot(adj_t[low, top], right[0]) + dot(adj_t[low, low], held), slots)
    exchange_start(3)
    own_v[1] = dot(adj_t[top, top], right[0]) + dot(adj_t[top, low], held)

    gather_wait(0, left.at[0], left.at[0])
    pre = dot(left[0, 0], w_v[0, block(0)])
    for h in range(1, hids):
        pre += dot(left[0, h], w_v[0, block(h)])
    pre_v[...] = pre

    left[1, hid] = (own_v[0] + dot(onehot_t[...], exchange_wait(2))).astype(BF)
    gather_start(1, left.at[1, hid], left.at[1, hid])
    right[1] = (own_v[1] + dot(onehot_t[...], exchange_wait(3))).astype(BF)
    for h in range(hids):
        rs_send[h] = (back_f32[h] + dot_r(right[1], w_v[3, block(h)])).astype(BF)
    for i in range(1, hids):
        peer = lax.rem(hid + i, hids)
        remote(rs_send.at[peer], rs_recv.at[hid], ysem.at[2], yrsem.at[2], hid=peer).start()

    gather_wait(1, left.at[1], left.at[1])
    pre = pre_v[...]
    for h in range(hids):
        pre += dot(left[1, h], w_v[2, block(h)])
    sigma = jax.nn.sigmoid(pre)
    hid_all[hid] = (pre * sigma).astype(BF)
    gather_start(3, hid_all.at[hid], hid_all.at[hid])
    send[4] = pack(dot(onehot[...], hid_all[hid]), slots)
    exchange_start(4)

    gather_wait(2, rs_send, rs_recv)
    back_one = rs_send[hid].astype(F32)
    for i in range(1, hids):
        back_one += rs_recv[lax.rem(hid + i, hids)].astype(F32)
    back_pre = (back_one * sigma * (1.0 + pre * (1.0 - sigma))).astype(BF)

    sibling = me + 1 - 2 * core
    piece = width // chips_x
    chunk = piece // chips_z
    factor = 1.0 / math.sqrt(doms * masters)
    z_order = sorted(range(chips_z), key=lambda j: -min(j, chips_z - j))

    def dom_of(x, z):
        return (x * chips_z + z) * 2 + core

    def to_sibling(g):
        return remote(s0s.at[g], s0r.at[g], gsem.at[g, 0], cr_sem.at[g], dom=sibling)

    def x_start(g):
        done = to_sibling(g)
        done.wait_recv()
        done.wait_send()
        s1s[g] = (acc[g] + s0r[g].astype(F32)).astype(BF)
        for j in z_order:
            rows = lax.rem(cz + j, chips_z) * chunk
            for i in range(1, chips_x):
                px = lax.rem(cx + i, chips_x)
                remote(
                    s1s.at[g, pl.ds(px * piece + rows, chunk)],
                    s1r.at[g, j, cx],
                    gsem.at[g, 1],
                    xr_sem.at[g, j],
                    dom=dom_of(px, cz),
                ).start()

    def z_start(g):
        for j in z_order:
            pz = lax.rem(cz + j, chips_z)
            some = s1r.at[g, j, pl.ds(0, chips_x - 1)]
            remote(some, some, gsem.at[g, 1], xr_sem.at[g, j], dom=sibling).wait_recv()
            mine = pl.ds(cx * piece + pz * chunk, chunk)
            total = acc[g, mine] + s0r[g, mine].astype(F32)
            for i in range(1, chips_x):
                total += s1r[g, j, lax.rem(cx + i, chips_x)].astype(F32)
            if j == 0:
                acc[g, mine] = total
                continue
            s2s[g, j] = total.astype(BF)
            remote(
                s2s.at[g, j], s2r.at[g, cz], gsem.at[g, 2], zr_sem.at[g], dom=dom_of(cx, pz)
            ).start()

    def chunk_at(g, x, z):
        return gout.at[g, core, pl.ds(x * piece + z * chunk, chunk)]

    def finish(g):
        some = s2r.at[g, pl.ds(0, chips_z - 1)]
        remote(some, some, gsem.at[g, 2], zr_sem.at[g], dom=sibling).wait_recv()
        total = acc[g, pl.ds(cx * piece + cz * chunk, chunk)]
        for i in range(1, chips_z):
            total += s2r[g, lax.rem(cz + i, chips_z)].astype(F32)
        fin[g] = (total * factor).astype(BF)
        place = chunk_at(g, cx, cz)
        for j in z_order:
            if j:
                pz = lax.rem(cz + j, chips_z)
                remote(fin.at[g], place, gsem.at[g, 3], za_sem.at[g, j], dom=dom_of(cx, pz)).start()
        for i in range(1, chips_x):
            px = lax.rem(cx + i, chips_x)
            remote(fin.at[g], place, gsem.at[g, 4], xa_sem.at[g], dom=dom_of(px, cz)).start()
        pltpu.make_async_copy(fin.at[g], place, lsem.at[7 + g]).start()

    def forward(g):
        for j in reversed(z_order):
            if j:
                place = chunk_at(g, cx, lax.rem(cz + chips_z - j, chips_z))
                remote(place, place, gsem.at[g, 3], za_sem.at[g, j], dom=sibling).wait_recv()
                for i in range(1, chips_x):
                    px = lax.rem(cx + i, chips_x)
                    remote(place, place, gsem.at[g, 4], xa_sem.at[g], dom=dom_of(px, cz)).start()

    def core_back(g):
        place = chunk_at(g, cx, cz)
        pltpu.make_async_copy(fin.at[g], place, lsem.at[7 + g]).wait()
        some = gout.at[g, core, pl.ds(0, (chips_x - 1) * piece)]
        remote(some, some, gsem.at[g, 4], xa_sem.at[g], dom=sibling).wait_recv()
        mine = gout.at[g, core]
        remote(mine, mine, gsem.at[g, 5], ca_sem.at[g], dom=sibling).start()

    def drain(g):
        def sent(stage, ref):
            remote(ref, ref, gsem.at[g, stage], ca_sem.at[g], dom=sibling).wait_send()

        most = (chips_x - 1) * piece
        sent(1, s1s.at[g, pl.ds(0, most)])
        sent(2, s2s.at[g, pl.ds(0, chips_z - 1)])
        sent(3, s2s.at[g, pl.ds(0, chips_z - 1)])
        sent(4, s1s.at[g, pl.ds(0, most)])
        mine = gout.at[g, core]
        done = remote(mine, mine, gsem.at[g, 5], ca_sem.at[g], dom=sibling)
        done.wait_recv()
        done.wait_send()

    for h in range(hids):
        s0s[0, block(h)] = dot_t(left[1 - core, h], back_pre).astype(BF)
    to_sibling(0).start()
    for h in range(hids):
        acc[0, block(h)] = dot_t(left[core, h], back_pre)
    x_start(0)
    held = exchange_wait(4)
    send[5] = pack(dot(adj[low, top], hid_all[hid]) + dot(adj[low, low], held), slots)
    exchange_start(5)
    own_v[0] = dot(adj[top, top], hid_all[hid]) + dot(adj[top, low], held)
    gather_wait(3, hid_all, hid_all)
    for h in range(hids):
        s0s[1, block(h)] = dot_t(hid_all[h], right[1 - core]).astype(BF)
    to_sibling(1).start()
    for h in range(hids):
        acc[1, block(h)] = dot_t(hid_all[h], right[core])
    x_start(1)
    z_start(0)
    finish(0)
    total = dot(hid_all[0], w_v[1, block(0)])
    for h in range(1, hids):
        total += dot(hid_all[h], w_v[1, block(h)])
    pre_v[...] = total
    z_start(1)
    forward(0)
    agg_two[hid] = (own_v[0] + dot(onehot_t[...], exchange_wait(5))).astype(BF)
    gather_start(4, agg_two.at[hid], agg_two.at[hid])
    finish(1)
    core_back(0)
    forward(1)
    gather_wait(4, agg_two, agg_two)
    total = pre_v[...]
    for h in range(hids):
        total += dot(agg_two[h], w_v[3, block(h)])
    out[...] = total.astype(BF)
    core_back(1)
    drain(0)
    drain(1)


def local(
    feat,
    cotangent,
    tiles,
    tile_index,
    tile_count,
    replica_slot,
    recv_count,
    w_self1,
    w_neigh1,
    w_self2,
    w_neigh2,
):
    doms, hids = lax.axis_size("dom"), lax.axis_size("hid")
    masters, narrow = feat.shape
    width = narrow * hids
    mirrors = replica_slot.shape[1]
    slots = mirrors // doms
    size = tiles.shape[2]
    blocks = (masters + mirrors) // size
    side = blocks * size
    chips_x = doms // (2 * CHIPS_Z)
    piece = width // chips_x
    chunk = piece // CHIPS_Z

    packed = slots * narrow // LANES
    smem = pl.BlockSpec(memory_space=pltpu.SMEM)
    vmem = pl.BlockSpec(memory_space=pltpu.VMEM)
    anym = pl.BlockSpec(memory_space=pl.ANY)
    hbm = pl.BlockSpec(memory_space=pltpu.HBM)
    dma = pltpu.SemaphoreType.DMA

    def body(*refs):
        kernel((doms, hids, slots, masters, narrow), *refs)

    out, grads = pl.pallas_call(
        body,
        out_shape=(
            jax.ShapeDtypeStruct((masters, narrow), BF),
            jax.ShapeDtypeStruct((2, 2, width, narrow), BF),
        ),
        in_specs=[smem] * 2 + [hbm] * 2 + [vmem] * 2 + [hbm] * 5,
        out_specs=(vmem, anym),
        scratch_shapes=[
            pltpu.VMEM(tiles.shape[1:], BF),
            pltpu.VMEM((4, width, narrow), BF),
            pltpu.VMEM((mirrors, masters), BF),
            pltpu.VMEM((masters, mirrors), BF),
            pltpu.VMEM((side, side), BF),
            pltpu.VMEM((side, side), BF),
            pltpu.VMEM((6, doms, packed, LANES), BF),
            pltpu.VMEM((6, doms, packed, LANES), BF),
            pltpu.VMEM((2, hids, masters, narrow), BF),
            pltpu.VMEM((hids, masters, narrow), BF),
            pltpu.VMEM((hids, masters, narrow), BF),
            pltpu.VMEM((2, masters, narrow), BF),
            pltpu.VMEM((hids, masters, narrow), F32),
            pltpu.VMEM((hids, masters, narrow), BF),
            pltpu.VMEM((hids, masters, narrow), BF),
            pltpu.VMEM((masters, narrow), F32),
            pltpu.VMEM((2, masters, narrow), F32),
            pltpu.VMEM((2, width, narrow), F32),
            pltpu.VMEM((2, width, narrow), BF),
            pltpu.VMEM((2, width, narrow), BF),
            pltpu.VMEM((2, width, narrow), BF),
            pltpu.VMEM((2, CHIPS_Z, chips_x, chunk, narrow), BF),
            pltpu.VMEM((2, CHIPS_Z, chunk, narrow), BF),
            pltpu.VMEM((2, CHIPS_Z, chunk, narrow), BF),
            pltpu.VMEM((2, chunk, narrow), BF),
            dma((9,)),
            dma((6,)),
            dma((6,)),
            dma((5,)),
            dma((5,)),
            dma((2, 6)),
            dma((2,)),
            dma((2, CHIPS_Z)),
            dma((2,)),
            dma((2, CHIPS_Z)),
            dma((2,)),
            dma((2,)),
        ],
        compiler_params=pltpu.CompilerParams(
            collective_id=0, has_side_effects=True, vmem_limit_bytes=60 * 1024 * 1024
        ),
    )(
        tile_index,
        tile_count,
        feat,
        cotangent,
        replica_slot,
        recv_count,
        tiles[0],
        w_self1,
        w_neigh1,
        w_self2,
        w_neigh2,
    )
    return (out, *(grads[i // 2, i % 2].astype(F32) for i in range(4)))


def solution(mesh):
    rows = P("dom", "hid")
    cols = P(None, "hid")
    return jax.shard_map(
        local,
        mesh=mesh,
        in_specs=(
            rows,
            rows,
            P("dom", None, None, None),
            P("dom", None),
            P("dom"),
            P("dom", None),
            P("dom", None),
            cols,
            cols,
            cols,
            cols,
        ),
        out_specs=(rows, cols, cols, cols, cols),
        check_vma=False,
    )
```

```python
import math

import jax
import jax.numpy as jnp
from jax import lax
from jax.experimental import pallas as pl
from jax.experimental.pallas import tpu as pltpu
from jax.sharding import PartitionSpec as P

BF = jnp.bfloat16
F32 = jnp.float32
I32 = jnp.int32
LANES = 128
CHIPS_Z = 8


def dot(a, b):
    return jnp.dot(a, b, preferred_element_type=F32)


def dot_t(a, b):
    return lax.dot_general(a, b, (((0,), (0,)), ((), ())), preferred_element_type=F32)


def dot_r(a, b):
    return lax.dot_general(a, b, (((1,), (1,)), ((), ())), preferred_element_type=F32)


def sum_groups(width):
    half = width // 2
    return tuple((m, base, half, True) for m in range(2) for base in (0, half))


def pack(rows, slots):
    count, width = rows.shape
    parts = [
        rows[:, i : i + LANES].reshape(count // slots, slots, LANES) for i in range(0, width, LANES)
    ]
    return jnp.concatenate(parts, axis=1).astype(BF)


def unpack(packed, slots):
    wide = packed.astype(F32)
    groups, rows, _ = wide.shape
    parts = [
        wide[:, i : i + slots, :].reshape(groups * slots, LANES) for i in range(0, rows, slots)
    ]
    return jnp.concatenate(parts, axis=1).astype(BF)


def kernel(
    dims,
    tile_at,
    tile_total,
    feat,
    cot,
    slot_row,
    counts,
    tiles,
    ws1,
    wn1,
    ws2,
    wn2,
    out,
    gout,
    tiles_v,
    w_v,
    onehot,
    onehot_t,
    adj,
    adj_t,
    send,
    recv,
    left,
    hid_all,
    agg_two,
    right,
    back_f32,
    rs_send,
    rs_recv,
    pre_v,
    own_v,
    acc,
    s0s,
    s0r,
    s1s,
    lsem,
    esem,
    ersem,
    ysem,
    yrsem,
    csem,
    gsem,
    cr_sem,
    xr_sem,
    zr_sem,
    za_sem,
    xa_sem,
    ca_sem,
    *bufs,
):
    doms, hids, slots, masters, narrow = dims
    chips_z = CHIPS_Z
    chips_x = doms // (2 * chips_z)
    size = tiles.shape[1]
    mirrors = doms * slots
    blocks = (masters + mirrors) // size
    width = hids * narrow
    me = lax.axis_index("dom")
    hid = lax.axis_index("hid")
    core = lax.rem(me, 2)
    chip = me // 2
    cx, cz = chip // chips_z, lax.rem(chip, chips_z)

    def remote(src, dst, ssem, rsem, **where):
        return pltpu.make_async_remote_copy(
            src_ref=src,
            dst_ref=dst,
            send_sem=ssem,
            recv_sem=rsem,
            device_id=where,
            device_id_type=pl.DeviceIdType.MESH,
        )

    barrier = pltpu.get_barrier_semaphore()

    def greet(i, carry):
        pl.semaphore_signal(
            barrier,
            inc=1,
            device_id={"dom": lax.rem(me + i, doms)},
            device_id_type=pl.DeviceIdType.MESH,
        )
        return carry

    lax.fori_loop(1, doms, greet, 0)
    for i in range(1, hids):
        pl.semaphore_signal(
            barrier,
            inc=1,
            device_id={"hid": lax.rem(hid + i, hids)},
            device_id_type=pl.DeviceIdType.MESH,
        )

    mine_in = left.at[0, hid]
    loads = [
        pltpu.make_async_copy(src, dst, lsem.at[i])
        for i, (src, dst) in enumerate(
            (
                (feat, mine_in),
                (cot, right.at[0]),
                (tiles, tiles_v),
                (ws2, w_v.at[1]),
                (ws1, w_v.at[0]),
                (wn1, w_v.at[2]),
                (wn2, w_v.at[3]),
            )
        )
    ]
    for load in loads:
        load.start()

    grp = lax.broadcasted_iota(I32, (doms, mirrors), 0)
    col = lax.broadcasted_iota(I32, (doms, mirrors), 1)
    repeat = (col // slots == grp).astype(F32)
    live_count = dot(jnp.broadcast_to(counts[...].astype(F32), (8, doms)), repeat)[0:1]
    lane = lax.broadcasted_iota(I32, (1, mirrors), 1)
    live = lax.rem(lane, slots).astype(F32) + 0.5 < live_count
    slot = jnp.where(live, slot_row[...], -1)
    row = lax.broadcasted_iota(I32, (masters, mirrors), 0)
    hot = (row == slot).astype(F32)
    onehot_t[...] = hot.astype(BF)
    onehot[...] = hot.T.astype(BF)

    loads[0].wait()
    send[0] = pack(dot(onehot[...], mine_in[...]), slots)
    for n in range(recv.shape[0]):
        recv[n, me] = jnp.zeros(recv.shape[2:], BF)

    pl.semaphore_wait(barrier, doms - 1 + hids - 1)

    def exchange_start(n):
        def one(i, carry):
            peer = lax.rem(me + i, doms)
            remote(send.at[n, peer], recv.at[n, me], esem.at[n], ersem.at[n], dom=peer).start()
            return carry

        near = doms // 3
        lax.fori_loop(near, doms, one, 0)
        lax.fori_loop(1, near, one, 0)

    def exchange_wait(n):
        some = pl.ds(0, doms - 1)
        done = remote(
            send.at[n, some], recv.at[n, some], esem.at[n], ersem.at[n], dom=lax.rem(me + 1, doms)
        )
        done.wait_recv()
        done.wait_send()
        return unpack(recv[n], slots)

    def gather_start(n, src, dst):
        for i in range(1, hids):
            remote(src, dst, ysem.at[n], yrsem.at[n], hid=lax.rem(hid + i, hids)).start()

    def gather_wait(n, src, dst):
        some = pl.ds(0, hids - 1)
        done = remote(src.at[some], dst.at[some], ysem.at[n], yrsem.at[n], hid=lax.rem(hid + 1, hids))
        done.wait_recv()
        done.wait_send()

    exchange_start(0)
    loads[1].wait()
    send[1] = pack(dot(onehot[...], right[0]), slots)
    exchange_start(1)
    gather_start(0, mine_in, mine_in)

    loads[2].wait()
    total_tiles = tile_total[0]
    for r in range(blocks):
        for c in range(blocks):
            e = r * blocks + c
            found = jnp.int32(0)
            for t in range(tiles.shape[0]):
                hit = jnp.logical_and(tile_at[0, t] == e, t < total_tiles)
                found = jnp.where(hit, t + 1, found)
            tile = jnp.where(found > 0, tiles_v[jnp.maximum(found - 1, 0)], jnp.zeros((), BF))
            rs, cs = pl.ds(r * size, size), pl.ds(c * size, size)
            adj[rs, cs] = tile
            adj_t[cs, rs] = tile.astype(F32).T.astype(BF)

    for load in loads[3:]:
        load.wait()

    def block(h):
        return pl.ds(h * narrow, narrow)

    for h in range(hids):
        back_f32[h] = dot_r(right[0], w_v[1, block(h)])

    top, low = pl.ds(0, masters), pl.ds(masters, mirrors)
    held = exchange_wait(0)
    send[2] = pack(dot(adj[low, top], mine_in[...]) + dot(adj[low, low], held), slots)
    exchange_start(2)
    own_v[0] = dot(adj[top, top], mine_in[...]) + dot(adj[top, low], held)

    held = exchange_wait(1)
    send[3] = pack(dot(adj_t[low, top], right[0]) + dot(adj_t[low, low], held), slots)
    exchange_start(3)
    own_v[1] = dot(adj_t[top, top], right[0]) + dot(adj_t[top, low], held)

    gather_wait(0, left.at[0], left.at[0])
    pre = dot(left[0, 0], w_v[0, block(0)])
    for h in range(1, hids):
        pre += dot(left[0, h], w_v[0, block(h)])
    pre_v[...] = pre

    left[1, hid] = (own_v[0] + dot(onehot_t[...], exchange_wait(2))).astype(BF)
    gather_start(1, left.at[1, hid], left.at[1, hid])
    right[1] = (own_v[1] + dot(onehot_t[...], exchange_wait(3))).astype(BF)
    for h in range(hids):
        rs_send[h] = (back_f32[h] + dot_r(right[1], w_v[3, block(h)])).astype(BF)
    for i in range(1, hids):
        peer = lax.rem(hid + i, hids)
        remote(rs_send.at[peer], rs_recv.at[hid], ysem.at[2], yrsem.at[2], hid=peer).start()

    gather_wait(1, left.at[1], left.at[1])
    pre = pre_v[...]
    for h in range(hids):
        pre += dot(left[1, h], w_v[2, block(h)])
    sigma = jax.nn.sigmoid(pre)
    hid_all[hid] = (pre * sigma).astype(BF)
    gather_start(3, hid_all.at[hid], hid_all.at[hid])
    send[4] = pack(dot(onehot[...], hid_all[hid]), slots)
    exchange_start(4)

    gather_wait(2, rs_send, rs_recv)
    back_one = rs_send[hid].astype(F32)
    for i in range(1, hids):
        back_one += rs_recv[lax.rem(hid + i, hids)].astype(F32)
    back_pre = (back_one * sigma * (1.0 + pre * (1.0 - sigma))).astype(BF)

    sibling = me + 1 - 2 * core
    factor = 1.0 / math.sqrt(doms * masters)

    def far_first(n):
        return sorted(range(n), key=lambda j: -min(j, n - j))

    class Sum:
        def __init__(self, g, m, base, rows, x_first, bufs):
            self.g, self.m, self.base, self.rows, self.x_first = g, m, base, rows, x_first
            self.n1, self.n2 = (chips_x, chips_z) if x_first else (chips_z, chips_x)
            self.c1, self.c2 = (cx, cz) if x_first else (cz, cx)
            self.piece = rows // self.n1
            self.chunk = self.piece // self.n2
            self.order = far_first(self.n2)
            self.r1, self.s2, self.r2, self.fin = bufs

        def dom_at(self, i1, i2):
            x, z = (i1, i2) if self.x_first else (i2, i1)
            return (x * chips_z + z) * 2 + core

        def rows_at(self, i1, i2):
            return pl.ds(self.base + i1 * self.piece + i2 * self.chunk, self.chunk)

        def other1(self, i):
            return lax.rem(self.c1 + i, self.n1)

        def other2(self, j):
            return lax.rem(self.c2 + j, self.n2)

        def place(self, i1, i2):
            return gout.at[self.m, core, self.rows_at(i1, i2)]

        def await_recv(self, sem, chunks):
            ref = s1s.at[self.m, pl.ds(0, chunks * self.chunk)]
            remote(ref, ref, gsem.at[self.g, 0], sem, dom=sibling).wait_recv()

        def core_copy(self):
            part = pl.ds(self.base, self.rows)
            return remote(
                s0s.at[self.m, part],
                s0r.at[self.m, part],
                csem.at[self.g],
                cr_sem.at[self.g],
                dom=sibling,
            )

        def first_start(self):
            done = self.core_copy()
            done.wait_recv()
            done.wait_send()
            part = pl.ds(self.base, self.rows)
            s1s[self.m, part] = (acc[self.m, part] + s0r[self.m, part].astype(F32)).astype(BF)
            for j in self.order:
                for i in range(1, self.n1):
                    remote(
                        s1s.at[self.m, self.rows_at(self.other1(i), self.other2(j))],
                        self.r1.at[j, self.c1],
                        gsem.at[self.g, 0],
                        xr_sem.at[self.g, j],
                        dom=self.dom_at(self.other1(i), self.c2),
                    ).start()

        def second_start(self):
            for j in self.order:
                self.await_recv(xr_sem.at[self.g, j], self.n1 - 1)
                part = self.rows_at(self.c1, self.other2(j))
                total = acc[self.m, part] + s0r[self.m, part].astype(F32)
                for i in range(1, self.n1):
                    total += self.r1[j, self.other1(i)].astype(F32)
                if j == 0:
                    acc[self.m, part] = total
                    continue
                self.s2[j] = total.astype(BF)
                remote(
                    self.s2.at[j],
                    self.r2.at[self.c2],
                    gsem.at[self.g, 1],
                    zr_sem.at[self.g],
                    dom=self.dom_at(self.c1, self.other2(j)),
                ).start()

        def along_first(self, src, place):
            for i in range(1, self.n1):
                remote(
                    src,
                    place,
                    gsem.at[self.g, 3],
                    xa_sem.at[self.g],
                    dom=self.dom_at(self.other1(i), self.c2),
                ).start()

        def finish(self):
            self.await_recv(zr_sem.at[self.g], self.n2 - 1)
            total = acc[self.m, self.rows_at(self.c1, self.c2)]
            for j in range(1, self.n2):
                total += self.r2[self.other2(j)].astype(F32)
            self.fin[...] = (total * factor).astype(BF)
            place = self.place(self.c1, self.c2)
            for j in self.order:
                if j:
                    remote(
                        self.fin,
                        place,
                        gsem.at[self.g, 2],
                        za_sem.at[self.g, j],
                        dom=self.dom_at(self.c1, self.other2(j)),
                    ).start()
            self.along_first(self.fin, place)
            pltpu.make_async_copy(self.fin, place, lsem.at[7 + self.g]).start()

        def forward(self):
            for j in reversed(self.order):
                if j:
                    place = self.place(self.c1, lax.rem(self.c2 + self.n2 - j, self.n2))
                    self.await_recv(za_sem.at[self.g, j], 1)
                    self.along_first(place, place)

        def sibling_copy(self):
            mine = gout.at[self.m, core, pl.ds(self.base, self.rows)]
            return remote(mine, mine, gsem.at[self.g, 4], ca_sem.at[self.g], dom=sibling)

        def core_back(self):
            place = self.place(self.c1, self.c2)
            pltpu.make_async_copy(self.fin, place, lsem.at[7 + self.g]).wait()
            self.await_recv(xa_sem.at[self.g], (self.n1 - 1) * self.n2)
            self.sibling_copy().start()

        def drain(self):
            along1, along2 = (self.n1 - 1) * self.n2, self.n2 - 1
            for stage, chunks in enumerate((along1, along2, along2, along1)):
                ref = s1s.at[self.m, pl.ds(0, chunks * self.chunk)]
                remote(ref, ref, gsem.at[self.g, stage], ca_sem.at[self.g], dom=sibling).wait_send()
            done = self.sibling_copy()
            done.wait_recv()
            done.wait_send()

    sums = [
        Sum(g, *spec, bufs[4 * g : 4 * g + 4]) for g, spec in enumerate(sum_groups(width))
    ]

    early = [one for one in sums if one.m == 0]
    late = [one for one in sums if one.m == 1]

    def blocks_of(one):
        return range(one.base // narrow, (one.base + one.rows) // narrow)

    for one in early:
        for h in blocks_of(one):
            s0s[0, block(h)] = dot_t(left[1 - core, h], back_pre).astype(BF)
        one.core_copy().start()
    for h in range(hids):
        acc[0, block(h)] = dot_t(left[core, h], back_pre)
    for one in early:
        one.first_start()

    held = exchange_wait(4)
    send[5] = pack(dot(adj[low, top], hid_all[hid]) + dot(adj[low, low], held), slots)
    exchange_start(5)
    own_v[0] = dot(adj[top, top], hid_all[hid]) + dot(adj[top, low], held)

    gather_wait(3, hid_all, hid_all)
    for one in late:
        for h in blocks_of(one):
            s0s[1, block(h)] = dot_t(hid_all[h], right[1 - core]).astype(BF)
        one.core_copy().start()
    for h in range(hids):
        acc[1, block(h)] = dot_t(hid_all[h], right[core])
    for one in late:
        one.first_start()
    for one in early:
        one.second_start()
    for one in early:
        one.finish()
    total = dot(hid_all[0], w_v[1, block(0)])
    for h in range(1, hids):
        total += dot(hid_all[h], w_v[1, block(h)])
    pre_v[...] = total
    for one in late:
        one.second_start()
    for one in early:
        one.forward()
    agg_two[hid] = (own_v[0] + dot(onehot_t[...], exchange_wait(5))).astype(BF)
    gather_start(4, agg_two.at[hid], agg_two.at[hid])
    for one in late:
        one.finish()
    for one in late:
        one.forward()
    for one in early:
        one.core_back()
    gather_wait(4, agg_two, agg_two)
    total = pre_v[...]
    for h in range(hids):
        total += dot(agg_two[h], w_v[3, block(h)])
    out[...] = total.astype(BF)
    for one in late:
        one.core_back()
    for one in sums:
        one.drain()


def local(
    feat,
    cotangent,
    tiles,
    tile_index,
    tile_count,
    replica_slot,
    recv_count,
    w_self1,
    w_neigh1,
    w_self2,
    w_neigh2,
):
    doms, hids = lax.axis_size("dom"), lax.axis_size("hid")
    masters, narrow = feat.shape
    width = narrow * hids
    mirrors = replica_slot.shape[1]
    slots = mirrors // doms
    size = tiles.shape[2]
    blocks = (masters + mirrors) // size
    side = blocks * size
    chips_x = doms // (2 * CHIPS_Z)
    groups = sum_groups(width)
    count = len(groups)
    buffers = []
    for _, _, rows, x_first in groups:
        n1, n2 = (chips_x, CHIPS_Z) if x_first else (CHIPS_Z, chips_x)
        chunk = rows // (n1 * n2)
        buffers += [
            pltpu.VMEM((n2, n1, chunk, narrow), BF),
            pltpu.VMEM((n2, chunk, narrow), BF),
            pltpu.VMEM((n2, chunk, narrow), BF),
            pltpu.VMEM((chunk, narrow), BF),
        ]

    packed = slots * narrow // LANES
    smem = pl.BlockSpec(memory_space=pltpu.SMEM)
    vmem = pl.BlockSpec(memory_space=pltpu.VMEM)
    anym = pl.BlockSpec(memory_space=pl.ANY)
    hbm = pl.BlockSpec(memory_space=pltpu.HBM)
    dma = pltpu.SemaphoreType.DMA

    def body(*refs):
        kernel((doms, hids, slots, masters, narrow), *refs)

    out, grads = pl.pallas_call(
        body,
        out_shape=(
            jax.ShapeDtypeStruct((masters, narrow), BF),
            jax.ShapeDtypeStruct((2, 2, width, narrow), BF),
        ),
        in_specs=[smem] * 2 + [hbm] * 2 + [vmem] * 2 + [hbm] * 5,
        out_specs=(vmem, anym),
        scratch_shapes=[
            pltpu.VMEM(tiles.shape[1:], BF),
            pltpu.VMEM((4, width, narrow), BF),
            pltpu.VMEM((mirrors, masters), BF),
            pltpu.VMEM((masters, mirrors), BF),
            pltpu.VMEM((side, side), BF),
            pltpu.VMEM((side, side), BF),
            pltpu.VMEM((6, doms, packed, LANES), BF),
            pltpu.VMEM((6, doms, packed, LANES), BF),
            pltpu.VMEM((2, hids, masters, narrow), BF),
            pltpu.VMEM((hids, masters, narrow), BF),
            pltpu.VMEM((hids, masters, narrow), BF),
            pltpu.VMEM((2, masters, narrow), BF),
            pltpu.VMEM((hids, masters, narrow), F32),
            pltpu.VMEM((hids, masters, narrow), BF),
            pltpu.VMEM((hids, masters, narrow), BF),
            pltpu.VMEM((masters, narrow), F32),
            pltpu.VMEM((2, masters, narrow), F32),
            pltpu.VMEM((2, width, narrow), F32),
            pltpu.VMEM((2, width, narrow), BF),
            pltpu.VMEM((2, width, narrow), BF),
            pltpu.VMEM((2, width, narrow), BF),
            dma((7 + count,)),
            dma((6,)),
            dma((6,)),
            dma((5,)),
            dma((5,)),
            dma((count,)),
            dma((count, 5)),
            dma((count,)),
            dma((count, CHIPS_Z)),
            dma((count,)),
            dma((count, CHIPS_Z)),
            dma((count,)),
            dma((count,)),
            *buffers,
        ],
        compiler_params=pltpu.CompilerParams(
            collective_id=0, has_side_effects=True, vmem_limit_bytes=60 * 1024 * 1024
        ),
    )(
        tile_index,
        tile_count,
        feat,
        cotangent,
        replica_slot,
        recv_count,
        tiles[0],
        w_self1,
        w_neigh1,
        w_self2,
        w_neigh2,
    )
    return (out, *(grads[i // 2, i % 2].astype(F32) for i in range(4)))


def solution(mesh):
    rows = P("dom", "hid")
    cols = P(None, "hid")
    return jax.shard_map(
        local,
        mesh=mesh,
        in_specs=(
            rows,
            rows,
            P("dom", None, None, None),
            P("dom", None),
            P("dom"),
            P("dom", None),
            P("dom", None),
            cols,
            cols,
            cols,
            cols,
        ),
        out_specs=(rows, cols, cols, cols, cols),
        check_vma=False,
    )
```

```python
import math

import jax
import jax.numpy as jnp
from jax import lax
from jax.experimental import pallas as pl
from jax.experimental.pallas import tpu as pltpu
from jax.sharding import PartitionSpec as P

BF = jnp.bfloat16
F32 = jnp.float32
I32 = jnp.int32
LANES = 128
CHIPS_Z = 8


def dot(a, b):
    return jnp.dot(a, b, preferred_element_type=F32)


def dot_t(a, b):
    return lax.dot_general(a, b, (((0,), (0,)), ((), ())), preferred_element_type=F32)


def dot_r(a, b):
    return lax.dot_general(a, b, (((1,), (1,)), ((), ())), preferred_element_type=F32)


def sum_groups(width):
    half = width // 2
    return tuple((m, base, half, True) for m in range(2) for base in (0, half))


def pack(rows, slots):
    count, width = rows.shape
    parts = [
        rows[:, i : i + LANES].reshape(count // slots, slots, LANES) for i in range(0, width, LANES)
    ]
    return jnp.concatenate(parts, axis=1).astype(BF)


def unpack(packed, slots):
    wide = packed.astype(F32)
    groups, rows, _ = wide.shape
    parts = [
        wide[:, i : i + slots, :].reshape(groups * slots, LANES) for i in range(0, rows, slots)
    ]
    return jnp.concatenate(parts, axis=1).astype(BF)


def kernel(
    dims,
    tile_at,
    tile_total,
    feat,
    cot,
    slot_row,
    counts,
    tiles,
    ws1,
    wn1,
    ws2,
    wn2,
    out,
    gout,
    tiles_v,
    w_v,
    onehot,
    onehot_t,
    adj,
    adj_t,
    send,
    recv,
    left,
    hid_all,
    agg_two,
    right,
    back_f32,
    rs_send,
    rs_recv,
    pre_v,
    own_v,
    acc,
    s0s,
    s0r,
    s1s,
    lsem,
    esem,
    ersem,
    ysem,
    yrsem,
    csem,
    gsem,
    cr_sem,
    xr_sem,
    zr_sem,
    za_sem,
    xa_sem,
    ca_sem,
    *bufs,
):
    doms, hids, slots, masters, narrow = dims
    chips_z = CHIPS_Z
    chips_x = doms // (2 * chips_z)
    size = tiles.shape[1]
    mirrors = doms * slots
    blocks = (masters + mirrors) // size
    width = hids * narrow
    me = lax.axis_index("dom")
    hid = lax.axis_index("hid")
    core = lax.rem(me, 2)
    chip = me // 2
    cx, cz = chip // chips_z, lax.rem(chip, chips_z)

    def remote(src, dst, ssem, rsem, **where):
        return pltpu.make_async_remote_copy(
            src_ref=src,
            dst_ref=dst,
            send_sem=ssem,
            recv_sem=rsem,
            device_id=where,
            device_id_type=pl.DeviceIdType.MESH,
        )

    def far_first(n):
        return sorted(range(n), key=lambda j: -min(j, n - j))

    barrier = pltpu.get_barrier_semaphore()

    def greet(i, carry):
        pl.semaphore_signal(
            barrier,
            inc=1,
            device_id={"dom": lax.rem(me + i, doms)},
            device_id_type=pl.DeviceIdType.MESH,
        )
        return carry

    lax.fori_loop(1, doms, greet, 0)
    for i in range(1, hids):
        pl.semaphore_signal(
            barrier,
            inc=1,
            device_id={"hid": lax.rem(hid + i, hids)},
            device_id_type=pl.DeviceIdType.MESH,
        )

    mine_in = left.at[0, hid]
    loads = [
        pltpu.make_async_copy(src, dst, lsem.at[i])
        for i, (src, dst) in enumerate(
            (
                (feat, mine_in),
                (cot, right.at[0]),
                (tiles, tiles_v),
                (ws2, w_v.at[1]),
                (ws1, w_v.at[0]),
                (wn1, w_v.at[2]),
                (wn2, w_v.at[3]),
            )
        )
    ]
    for load in loads:
        load.start()

    grp = lax.broadcasted_iota(I32, (doms, mirrors), 0)
    col = lax.broadcasted_iota(I32, (doms, mirrors), 1)
    repeat = (col // slots == grp).astype(F32)
    live_count = dot(jnp.broadcast_to(counts[...].astype(F32), (8, doms)), repeat)[0:1]
    lane = lax.broadcasted_iota(I32, (1, mirrors), 1)
    live = lax.rem(lane, slots).astype(F32) + 0.5 < live_count
    slot = jnp.where(live, slot_row[...], -1)
    row = lax.broadcasted_iota(I32, (masters, mirrors), 0)
    hot = (row == slot).astype(F32)
    onehot_t[...] = hot.astype(BF)
    onehot[...] = hot.T.astype(BF)

    loads[0].wait()
    send[0] = pack(dot(onehot[...], mine_in[...]), slots)
    for n in range(recv.shape[0]):
        recv[n, me] = jnp.zeros(recv.shape[2:], BF)

    pl.semaphore_wait(barrier, doms - 1 + hids - 1)

    def exchange_start(n):
        def one(i, carry):
            peer = lax.rem(me + i, doms)
            remote(send.at[n, peer], recv.at[n, me], esem.at[n], ersem.at[n], dom=peer).start()
            return carry

        near = doms // 3
        lax.fori_loop(near, doms, one, 0)
        lax.fori_loop(1, near, one, 0)

    def exchange_wait(n):
        some = pl.ds(0, doms - 1)
        done = remote(
            send.at[n, some], recv.at[n, some], esem.at[n], ersem.at[n], dom=lax.rem(me + 1, doms)
        )
        done.wait_recv()
        done.wait_send()
        return unpack(recv[n], slots)

    def gather_start(n, src, dst):
        for i in far_first(hids)[:-1]:
            remote(src, dst, ysem.at[n], yrsem.at[n], hid=lax.rem(hid + i, hids)).start()

    def gather_wait(n, src, dst):
        some = pl.ds(0, hids - 1)
        done = remote(src.at[some], dst.at[some], ysem.at[n], yrsem.at[n], hid=lax.rem(hid + 1, hids))
        done.wait_recv()
        done.wait_send()

    exchange_start(0)
    loads[1].wait()
    send[1] = pack(dot(onehot[...], right[0]), slots)
    exchange_start(1)
    gather_start(0, mine_in, mine_in)

    loads[2].wait()
    total_tiles = tile_total[0]
    for r in range(blocks):
        for c in range(blocks):
            e = r * blocks + c
            found = jnp.int32(0)
            for t in range(tiles.shape[0]):
                hit = jnp.logical_and(tile_at[0, t] == e, t < total_tiles)
                found = jnp.where(hit, t + 1, found)
            tile = jnp.where(found > 0, tiles_v[jnp.maximum(found - 1, 0)], jnp.zeros((), BF))
            rs, cs = pl.ds(r * size, size), pl.ds(c * size, size)
            adj[rs, cs] = tile
            adj_t[cs, rs] = tile.astype(F32).T.astype(BF)

    for load in loads[3:]:
        load.wait()

    def block(h):
        return pl.ds(h * narrow, narrow)

    for h in range(hids):
        back_f32[h] = dot_r(right[0], w_v[1, block(h)])

    top, low = pl.ds(0, masters), pl.ds(masters, mirrors)
    held = exchange_wait(0)
    send[2] = pack(dot(adj[low, top], mine_in[...]) + dot(adj[low, low], held), slots)
    exchange_start(2)
    own_v[0] = dot(adj[top, top], mine_in[...]) + dot(adj[top, low], held)

    held = exchange_wait(1)
    send[3] = pack(dot(adj_t[low, top], right[0]) + dot(adj_t[low, low], held), slots)
    exchange_start(3)
    own_v[1] = dot(adj_t[top, top], right[0]) + dot(adj_t[top, low], held)

    gather_wait(0, left.at[0], left.at[0])
    pre = dot(left[0, 0], w_v[0, block(0)])
    for h in range(1, hids):
        pre += dot(left[0, h], w_v[0, block(h)])
    pre_v[...] = pre

    left[1, hid] = (own_v[0] + dot(onehot_t[...], exchange_wait(2))).astype(BF)
    gather_start(1, left.at[1, hid], left.at[1, hid])
    right[1] = (own_v[1] + dot(onehot_t[...], exchange_wait(3))).astype(BF)
    for h in range(hids):
        rs_send[h] = (back_f32[h] + dot_r(right[1], w_v[3, block(h)])).astype(BF)
    for i in far_first(hids)[:-1]:
        peer = lax.rem(hid + i, hids)
        remote(rs_send.at[peer], rs_recv.at[hid], ysem.at[2], yrsem.at[2], hid=peer).start()

    gather_wait(1, left.at[1], left.at[1])
    pre = pre_v[...]
    for h in range(hids):
        pre += dot(left[1, h], w_v[2, block(h)])
    sigma = jax.nn.sigmoid(pre)
    hid_all[hid] = (pre * sigma).astype(BF)
    gather_start(3, hid_all.at[hid], hid_all.at[hid])
    send[4] = pack(dot(onehot[...], hid_all[hid]), slots)
    exchange_start(4)

    gather_wait(2, rs_send, rs_recv)
    back_one = rs_send[hid].astype(F32)
    for i in range(1, hids):
        back_one += rs_recv[lax.rem(hid + i, hids)].astype(F32)
    back_pre = (back_one * sigma * (1.0 + pre * (1.0 - sigma))).astype(BF)

    sibling = me + 1 - 2 * core
    factor = 1.0 / math.sqrt(doms * masters)

    class Sum:
        def __init__(self, g, m, base, rows, x_first, bufs):
            self.g, self.m, self.base, self.rows, self.x_first = g, m, base, rows, x_first
            self.n1, self.n2 = (chips_x, chips_z) if x_first else (chips_z, chips_x)
            self.c1, self.c2 = (cx, cz) if x_first else (cz, cx)
            self.piece = rows // self.n1
            self.chunk = self.piece // self.n2
            self.order = far_first(self.n2)
            self.r1, self.s2, self.r2, self.fin = bufs

        def dom_at(self, i1, i2):
            x, z = (i1, i2) if self.x_first else (i2, i1)
            return (x * chips_z + z) * 2 + core

        def rows_at(self, i1, i2):
            return pl.ds(self.base + i1 * self.piece + i2 * self.chunk, self.chunk)

        def other1(self, i):
            return lax.rem(self.c1 + i, self.n1)

        def other2(self, j):
            return lax.rem(self.c2 + j, self.n2)

        def place(self, i1, i2):
            return gout.at[self.m, core, self.rows_at(i1, i2)]

        def await_recv(self, sem, chunks):
            ref = s1s.at[self.m, pl.ds(0, chunks * self.chunk)]
            remote(ref, ref, gsem.at[self.g, 0], sem, dom=sibling).wait_recv()

        def core_copy(self):
            part = pl.ds(self.base, self.rows)
            return remote(
                s0s.at[self.m, part],
                s0r.at[self.m, part],
                csem.at[self.g],
                cr_sem.at[self.g],
                dom=sibling,
            )

        def first_start(self):
            done = self.core_copy()
            done.wait_recv()
            done.wait_send()
            part = pl.ds(self.base, self.rows)
            s1s[self.m, part] = (acc[self.m, part] + s0r[self.m, part].astype(F32)).astype(BF)
            for j in self.order:
                for i in range(1, self.n1):
                    remote(
                        s1s.at[self.m, self.rows_at(self.other1(i), self.other2(j))],
                        self.r1.at[j, self.c1],
                        gsem.at[self.g, 0],
                        xr_sem.at[self.g, j],
                        dom=self.dom_at(self.other1(i), self.c2),
                    ).start()

        def second_start(self):
            for j in self.order:
                self.await_recv(xr_sem.at[self.g, j], self.n1 - 1)
                part = self.rows_at(self.c1, self.other2(j))
                total = acc[self.m, part] + s0r[self.m, part].astype(F32)
                for i in range(1, self.n1):
                    total += self.r1[j, self.other1(i)].astype(F32)
                if j == 0:
                    acc[self.m, part] = total
                    continue
                self.s2[j] = total.astype(BF)
                remote(
                    self.s2.at[j],
                    self.r2.at[self.c2],
                    gsem.at[self.g, 1],
                    zr_sem.at[self.g],
                    dom=self.dom_at(self.c1, self.other2(j)),
                ).start()

        def along_first(self, src, place):
            for i in range(1, self.n1):
                remote(
                    src,
                    place,
                    gsem.at[self.g, 3],
                    xa_sem.at[self.g],
                    dom=self.dom_at(self.other1(i), self.c2),
                ).start()

        def finish(self):
            self.await_recv(zr_sem.at[self.g], self.n2 - 1)
            total = acc[self.m, self.rows_at(self.c1, self.c2)]
            for j in range(1, self.n2):
                total += self.r2[self.other2(j)].astype(F32)
            self.fin[...] = (total * factor).astype(BF)
            place = self.place(self.c1, self.c2)
            for j in self.order:
                if j:
                    remote(
                        self.fin,
                        place,
                        gsem.at[self.g, 2],
                        za_sem.at[self.g, j],
                        dom=self.dom_at(self.c1, self.other2(j)),
                    ).start()
            self.along_first(self.fin, place)
            pltpu.make_async_copy(self.fin, place, lsem.at[7 + self.g]).start()

        def forward(self):
            for j in reversed(self.order):
                if j:
                    place = self.place(self.c1, lax.rem(self.c2 + self.n2 - j, self.n2))
                    self.await_recv(za_sem.at[self.g, j], 1)
                    self.along_first(place, place)

        def sibling_copy(self):
            mine = gout.at[self.m, core, pl.ds(self.base, self.rows)]
            return remote(mine, mine, gsem.at[self.g, 4], ca_sem.at[self.g], dom=sibling)

        def core_back(self):
            place = self.place(self.c1, self.c2)
            pltpu.make_async_copy(self.fin, place, lsem.at[7 + self.g]).wait()
            self.await_recv(xa_sem.at[self.g], (self.n1 - 1) * self.n2)
            self.sibling_copy().start()

        def drain(self):
            along1, along2 = (self.n1 - 1) * self.n2, self.n2 - 1
            for stage, chunks in enumerate((along1, along2, along2, along1)):
                ref = s1s.at[self.m, pl.ds(0, chunks * self.chunk)]
                remote(ref, ref, gsem.at[self.g, stage], ca_sem.at[self.g], dom=sibling).wait_send()
            done = self.sibling_copy()
            done.wait_recv()
            done.wait_send()

    sums = [
        Sum(g, *spec, bufs[4 * g : 4 * g + 4]) for g, spec in enumerate(sum_groups(width))
    ]

    early = [one for one in sums if one.m == 0]
    late = [one for one in sums if one.m == 1]

    def blocks_of(one):
        return range(one.base // narrow, (one.base + one.rows) // narrow)

    for one in early:
        for h in blocks_of(one):
            s0s[0, block(h)] = dot_t(left[1 - core, h], back_pre).astype(BF)
        one.core_copy().start()
    for h in range(hids):
        acc[0, block(h)] = dot_t(left[core, h], back_pre)
    for one in early:
        one.first_start()

    gather_wait(3, hid_all, hid_all)
    for one in late:
        for h in blocks_of(one):
            s0s[1, block(h)] = dot_t(hid_all[h], right[1 - core]).astype(BF)
        one.core_copy().start()
    for h in range(hids):
        acc[1, block(h)] = dot_t(hid_all[h], right[core])
    held = exchange_wait(4)
    send[5] = pack(dot(adj[low, top], hid_all[hid]) + dot(adj[low, low], held), slots)
    exchange_start(5)
    own_v[0] = dot(adj[top, top], hid_all[hid]) + dot(adj[top, low], held)

    for one in late:
        one.first_start()
    for one in early:
        one.second_start()
    for one in early:
        one.finish()
    total = dot(hid_all[0], w_v[1, block(0)])
    for h in range(1, hids):
        total += dot(hid_all[h], w_v[1, block(h)])
    pre_v[...] = total
    for one in late:
        one.second_start()
    for one in early:
        one.forward()
    for one in late:
        one.finish()
    agg_two[hid] = (own_v[0] + dot(onehot_t[...], exchange_wait(5))).astype(BF)
    gather_start(4, agg_two.at[hid], agg_two.at[hid])
    for one in late:
        one.forward()
    for one in early:
        one.core_back()
    gather_wait(4, agg_two, agg_two)
    total = pre_v[...]
    for h in range(hids):
        total += dot(agg_two[h], w_v[3, block(h)])
    out[...] = total.astype(BF)
    for one in late:
        one.core_back()
    for one in sums:
        one.drain()


def local(
    feat,
    cotangent,
    tiles,
    tile_index,
    tile_count,
    replica_slot,
    recv_count,
    w_self1,
    w_neigh1,
    w_self2,
    w_neigh2,
):
    doms, hids = lax.axis_size("dom"), lax.axis_size("hid")
    masters, narrow = feat.shape
    width = narrow * hids
    mirrors = replica_slot.shape[1]
    slots = mirrors // doms
    size = tiles.shape[2]
    blocks = (masters + mirrors) // size
    side = blocks * size
    chips_x = doms // (2 * CHIPS_Z)
    groups = sum_groups(width)
    count = len(groups)
    buffers = []
    for _, _, rows, x_first in groups:
        n1, n2 = (chips_x, CHIPS_Z) if x_first else (CHIPS_Z, chips_x)
        chunk = rows // (n1 * n2)
        buffers += [
            pltpu.VMEM((n2, n1, chunk, narrow), BF),
            pltpu.VMEM((n2, chunk, narrow), BF),
            pltpu.VMEM((n2, chunk, narrow), BF),
            pltpu.VMEM((chunk, narrow), BF),
        ]

    packed = slots * narrow // LANES
    smem = pl.BlockSpec(memory_space=pltpu.SMEM)
    vmem = pl.BlockSpec(memory_space=pltpu.VMEM)
    anym = pl.BlockSpec(memory_space=pl.ANY)
    hbm = pl.BlockSpec(memory_space=pltpu.HBM)
    dma = pltpu.SemaphoreType.DMA

    def body(*refs):
        kernel((doms, hids, slots, masters, narrow), *refs)

    out, grads = pl.pallas_call(
        body,
        out_shape=(
            jax.ShapeDtypeStruct((masters, narrow), BF),
            jax.ShapeDtypeStruct((2, 2, width, narrow), BF),
        ),
        in_specs=[smem] * 2 + [hbm] * 2 + [vmem] * 2 + [hbm] * 5,
        out_specs=(vmem, anym),
        scratch_shapes=[
            pltpu.VMEM(tiles.shape[1:], BF),
            pltpu.VMEM((4, width, narrow), BF),
            pltpu.VMEM((mirrors, masters), BF),
            pltpu.VMEM((masters, mirrors), BF),
            pltpu.VMEM((side, side), BF),
            pltpu.VMEM((side, side), BF),
            pltpu.VMEM((6, doms, packed, LANES), BF),
            pltpu.VMEM((6, doms, packed, LANES), BF),
            pltpu.VMEM((2, hids, masters, narrow), BF),
            pltpu.VMEM((hids, masters, narrow), BF),
            pltpu.VMEM((hids, masters, narrow), BF),
            pltpu.VMEM((2, masters, narrow), BF),
            pltpu.VMEM((hids, masters, narrow), F32),
            pltpu.VMEM((hids, masters, narrow), BF),
            pltpu.VMEM((hids, masters, narrow), BF),
            pltpu.VMEM((masters, narrow), F32),
            pltpu.VMEM((2, masters, narrow), F32),
            pltpu.VMEM((2, width, narrow), F32),
            pltpu.VMEM((2, width, narrow), BF),
            pltpu.VMEM((2, width, narrow), BF),
            pltpu.VMEM((2, width, narrow), BF),
            dma((7 + count,)),
            dma((6,)),
            dma((6,)),
            dma((5,)),
            dma((5,)),
            dma((count,)),
            dma((count, 5)),
            dma((count,)),
            dma((count, CHIPS_Z)),
            dma((count,)),
            dma((count, CHIPS_Z)),
            dma((count,)),
            dma((count,)),
            *buffers,
        ],
        compiler_params=pltpu.CompilerParams(
            collective_id=0, has_side_effects=True, vmem_limit_bytes=60 * 1024 * 1024
        ),
    )(
        tile_index,
        tile_count,
        feat,
        cotangent,
        replica_slot,
        recv_count,
        tiles[0],
        w_self1,
        w_neigh1,
        w_self2,
        w_neigh2,
    )
    return (out, *(grads[i // 2, i % 2].astype(F32) for i in range(4)))


def solution(mesh):
    rows = P("dom", "hid")
    cols = P(None, "hid")
    return jax.shard_map(
        local,
        mesh=mesh,
        in_specs=(
            rows,
            rows,
            P("dom", None, None, None),
            P("dom", None),
            P("dom"),
            P("dom", None),
            P("dom", None),
            cols,
            cols,
            cols,
            cols,
        ),
        out_specs=(rows, cols, cols, cols, cols),
        check_vma=False,
    )
```
